512 devices in a mesh: chol: 16 (over z_lo, x, core), occ: 32 (over y, z_hi).
Axes of the slice: x: 4, y: 8, z: 8 (z_hi: 4, z_lo: 2; z = z_hi * 2 + z_lo), core: 2. Of those that a mesh axis runs over, the one named last changes fastest.
Arguments:
- vectors: bfloat16 [128, 1536, 1536], P('chol', 'occ'), may hold values from -0.3984375 to 0.3984375
- coeffs: bfloat16 [2, 1536, 256], P(None, 'occ'), may hold values from -0.15625 to 0.15625
Outputs:
- exchange: float32 [2, 1536, 1536], P(None, 'occ', 'chol')
- coulomb: float32 [1536, 1536], P('occ', 'chol')
The draws below stay inside these ranges and needn't reach their ends.
All inputs are finite; a program needn't handle non-finite values.
Results may differ from the reference program's by a relative error of at most 0.0028.
Values may be sent and summed in bfloat16 or wider, within the bound.
No kernel may reach another device: no remote copies, remote signals or barrier semaphores. Data moves between devices by JAX's collectives and lax.ppermute only.
A program may use at most 128 MiB of HBM per device.

```python
import jax
import jax.numpy as jnp
from jax import lax

NAO = 1536
NOCC = 256
NCH = 128


def shard_levels(stream_key, extent, shards, least, high):
    loudness = 1.0
    for position, blocks in shards:
        draws = jax.random.uniform(jax.random.fold_in(jax.random.fold_in(stream_key, 6), position), (blocks,), jnp.float32, least / len(shards), high / len(shards))
        loudness = loudness * jnp.repeat(jnp.exp(draws), extent[position] // blocks).reshape((-1,) + (1,) * (len(extent) - 1 - position))
    return loudness


def centred(own_key, extent, spread, limit, pieces=(), dtype=jnp.bfloat16):
    array = spread * jax.random.normal(own_key, extent, jnp.float32)
    if pieces:
        array = array * shard_levels(own_key, extent, pieces, -0.22, 0.18)
    return jnp.clip(array, -limit, limit).astype(dtype)


def setup_inputs(seed: int = 0) -> dict:
    key_list = jax.random.split(jax.random.key(seed), 3)
    vectors = centred(key_list[0], (NCH, NAO, NAO), 0.0625, 0.3984375, ((0, 16), (1, 32)))
    coeffs = centred(key_list[1], (2, NAO, NOCC), NAO ** -0.5, 0.15625, ((1, 32),))
    return {"vectors": vectors, "coeffs": coeffs}


def reference(vectors, coeffs):
    wide_vectors = vectors.astype(jnp.float32)
    wide_coeffs = coeffs.astype(jnp.float32)
    half_slab = jnp.einsum("pnm,cmi->pcin", wide_vectors, wide_coeffs).astype(jnp.bfloat16)
    half_slab = lax.optimization_barrier(half_slab)
    slab_wide = half_slab.astype(jnp.float32)
    vector_weight = jnp.einsum("cni,pcin->p", wide_coeffs, slab_wide)
    real_part = jnp.einsum("pcim,pcin->mn", slab_wide, slab_wide)
    imag_part = jnp.einsum("pim,pin->mn", slab_wide[:, 1], slab_wide[:, 0]) - jnp.einsum("pim,pin->mn", slab_wide[:, 0], slab_wide[:, 1])
    exchange = jnp.stack([real_part, imag_part])
    coulomb = jnp.einsum("pmn,p->mn", wide_vectors, vector_weight)
    return exchange, coulomb
```

```python
import jax
import jax.numpy as jnp
from jax import lax
from jax.sharding import Mesh
from jax.sharding import PartitionSpec as P

NEAR = ("zl", "x")
FAR = ("y", "zb", "za")
SUMS = ("y", "za")
SWAP = [(0, 1), (1, 0)]


def to_all(block, axes, count):
    return lax.all_to_all(jnp.broadcast_to(block[None], (count,) + block.shape), axes, 0, 0, tiled=True)


def on_device(vectors, coeffs):
    f32, bf16 = jnp.float32, jnp.bfloat16
    core = lax.axis_index("core")
    zb = lax.axis_index("zb")
    count, rows, nao = vectors.shape
    half = coeffs.shape[2] // 2
    wide = 2 * half

    other_vectors = lax.ppermute(vectors, "core", SWAP)
    own = lax.dynamic_slice_in_dim(coeffs, core * half, half, 2)
    own = jnp.concatenate([own[0], own[1]], axis=1)
    full = to_all(own, FAR, 32).reshape(nao, wide)

    def transform(block):
        return jnp.dot(
            block.reshape(count * rows, nao), full, preferred_element_type=f32
        ).astype(bf16).reshape(count, rows, wide)

    mine, other = transform(vectors), transform(other_vectors)
    first = core == 0
    slab = jnp.concatenate([jnp.where(first, mine, other), jnp.where(first, other, mine)])

    terms = jnp.sum(slab.astype(f32) * own.astype(f32)[None], axis=(1, 2))
    terms = jnp.broadcast_to(terms[:, None], (16, 128))
    weights = jnp.sum(to_all(terms, ("core",) + FAR, 64), axis=0)[:, 0]
    weights = lax.dynamic_slice_in_dim(weights, core * count, count, 0)
    coulomb_part = jnp.sum(vectors.astype(f32) * weights[:, None, None], axis=0)
    coulomb_part = coulomb_part.reshape(rows, 16, nao // 16).transpose(1, 0, 2)
    coulomb = jnp.sum(lax.all_to_all(coulomb_part, NEAR + ("core",), 0, 0, tiled=True), axis=0)

    pieces = jnp.broadcast_to(slab.reshape(8, 1, 2, rows, wide), (8, 2, 2, rows, wide)).reshape(32, rows, wide)
    got = lax.all_to_all(pieces, FAR, 0, 0, tiled=True)
    got_other = lax.ppermute(got, "core", SWAP)

    def parts(block):
        block = block.reshape(8, 2, 2 * rows, wide)
        row_part = lax.dynamic_index_in_dim(block, zb, 1, keepdims=False)
        column_part = lax.dynamic_index_in_dim(block, core, 1, keepdims=False)
        return row_part.reshape(16 * rows, wide), column_part

    row_a, column_a = parts(got)
    row_b, column_b = parts(got_other)
    row_side = jnp.concatenate([row_a, row_b], axis=1)

    def turned(block):
        return jnp.concatenate([-block[..., half:], block[..., :half]], axis=-1)

    real = jnp.concatenate([column_a, column_b], axis=-1)
    imag = jnp.concatenate([turned(column_a), turned(column_b)], axis=-1)
    column_side = jnp.stack([real, imag], axis=1).reshape(32 * rows, 2 * wide)
    exchange = lax.dot_general(
        column_side, row_side, (((1,), (1,)), ((), ())), preferred_element_type=f32
    ).astype(bf16).reshape(8, 4 * rows, 16 * rows)
    exchange = jnp.sum(lax.all_to_all(exchange, NEAR, 0, 0, tiled=True).astype(f32), axis=0)
    exchange = exchange.astype(bf16).T.reshape(16, rows, 4 * rows)
    exchange = jnp.sum(lax.all_to_all(exchange, SUMS, 0, 0, tiled=True).astype(f32), axis=0)
    exchange = exchange.reshape(rows, 2, 2 * rows).transpose(1, 0, 2)
    return exchange, coulomb


def solution(mesh):
    fine = Mesh(mesh.devices.reshape(2, 4, 2, 8, 2, 2), ("zl", "x", "core", "y", "zb", "za"))
    chol = ("zl", "x", "core")
    return jax.shard_map(
        on_device,
        mesh=fine,
        in_specs=(P(chol, FAR, None), P(None, FAR, None)),
        out_specs=(P(None, FAR, chol), P(FAR, chol)),
        check_vma=False,
    )
```

```python
import jax
import jax.numpy as jnp
from jax import lax
from jax.sharding import Mesh
from jax.sharding import PartitionSpec as P

NEAR = ("zl", "x")
FAR = ("y", "zb", "za")
SUMS = ("y", "za")
SWAP = [(0, 1), (1, 0)]
f32, bf16 = jnp.float32, jnp.bfloat16


def words(value):
    high = lax.reduce_precision(value, 8, 7)
    return high.astype(bf16), (value - high).astype(bf16)


def on_device(vectors, coeffs):
    core = lax.axis_index("core")
    zb = lax.axis_index("zb")
    count, rows, nao = vectors.shape
    half = coeffs.shape[2] // 2
    wide = 2 * half

    other_vectors = lax.ppermute(vectors, "core", SWAP)
    own = lax.dynamic_slice_in_dim(coeffs, core * half, half, 2)
    own = jnp.concatenate([own[0], own[1]], axis=1)
    full = lax.all_to_all(jnp.broadcast_to(own[None], (32, rows, wide)), FAR, 0, 0, tiled=True)
    full = full.reshape(nao, wide)

    def transform(block):
        return jnp.dot(
            block.reshape(count * rows, nao), full, preferred_element_type=f32
        ).astype(bf16).reshape(count, rows, wide)

    mine, other = transform(vectors), transform(other_vectors)
    first = core == 0
    slab = jnp.concatenate([jnp.where(first, mine, other), jnp.where(first, other, mine)])

    terms = jnp.sum(slab.astype(f32) * own.astype(f32)[None], axis=(1, 2))
    high, low = words(terms)
    terms = jnp.concatenate([high, low, jnp.zeros((wide - 32,), bf16)])
    terms = jnp.concatenate([terms[None], jnp.zeros((7, wide), bf16)])
    terms = jnp.broadcast_to(terms[None], (16, 8, wide))
    pieces = jnp.concatenate([slab, terms], axis=1).reshape(8, 1, 2, rows + 8, wide)
    pieces = jnp.broadcast_to(pieces, (8, 2, 2, rows + 8, wide)).reshape(32, rows + 8, wide)
    got = lax.all_to_all(pieces, FAR, 0, 0, tiled=True)
    got_other = lax.ppermute(got, "core", SWAP)

    weights = jnp.sum((got[:, rows] + 0.0).astype(f32) + got_other[:, rows].astype(f32), axis=0)
    weights = weights[:16] + weights[16:32]
    mine_weights = lax.dynamic_slice_in_dim(weights, core * count, count, 0)
    other_weights = lax.dynamic_slice_in_dim(weights, (1 - core) * count, count, 0)
    coulomb = jnp.sum(
        vectors.astype(f32) * mine_weights[:, None, None]
        + other_vectors.astype(f32) * other_weights[:, None, None],
        axis=0,
    )
    coulomb = lax.dynamic_index_in_dim(coulomb.reshape(rows, 8, 2, 2 * rows), core, 2, keepdims=False)
    high, low = words(coulomb)
    coulomb = jnp.stack([high, low]).transpose(2, 0, 1, 3).reshape(8, 12, 16 * rows)
    coulomb = jnp.pad(coulomb, ((0, 0), (0, 4), (0, 0)))

    def parts(block):
        block = block[:, :rows].reshape(8, 2, 2 * rows, wide)
        row_part = lax.dynamic_index_in_dim(block, zb, 1, keepdims=False)
        column_part = lax.dynamic_index_in_dim(block, core, 1, keepdims=False)
        return row_part.reshape(16 * rows, wide), column_part

    row_a, column_a = parts(got)
    row_b, column_b = parts(got_other)
    row_side = jnp.concatenate([row_a, row_b], axis=1)

    def turned(block):
        return jnp.concatenate([-block[..., half:], block[..., :half]], axis=-1)

    real = jnp.concatenate([column_a, column_b], axis=-1)
    imag = jnp.concatenate([turned(column_a), turned(column_b)], axis=-1)
    column_side = jnp.stack([real, imag], axis=1).reshape(32 * rows, 2 * wide)
    exchange = lax.dot_general(
        column_side, row_side, (((1,), (1,)), ((), ())), preferred_element_type=f32
    ).astype(bf16).reshape(8, 4 * rows, 16 * rows)
    sums = lax.all_to_all(jnp.concatenate([exchange, coulomb], axis=1), NEAR, 0, 0, tiled=True)
    sums = jnp.sum(sums.astype(f32), axis=0)
    coulomb = sums[4 * rows : 4 * rows + 12].reshape(2, rows, 2 * rows)
    coulomb = coulomb[0] + coulomb[1]
    exchange = sums[: 4 * rows].astype(bf16).T.reshape(16, rows, 4 * rows)
    exchange = jnp.sum(lax.all_to_all(exchange, SUMS, 0, 0, tiled=True).astype(f32), axis=0)
    exchange = exchange.reshape(rows, 2, 2 * rows).transpose(1, 0, 2)
    return exchange, coulomb


def solution(mesh):
    fine = Mesh(mesh.devices.reshape(2, 4, 2, 8, 2, 2), ("zl", "x", "core", "y", "zb", "za"))
    chol = ("zl", "x", "core")
    return jax.shard_map(
        on_device,
        mesh=fine,
        in_specs=(P(chol, FAR, None), P(None, FAR, None)),
        out_specs=(P(None, FAR, chol), P(FAR, chol)),
        check_vma=False,
    )
```

```python
import jax
import jax.numpy as jnp
from jax import lax
from jax.experimental import pallas as pl
from jax.experimental.pallas import tpu as pltpu
from jax.sharding import Mesh
from jax.sharding import PartitionSpec as P

NEAR = ("zl", "x")
FAR = ("y", "zb", "za")
SUMS = ("y", "za")
SWAP = [(0, 1), (1, 0)]
f32, bf16 = jnp.float32, jnp.bfloat16
SMEM = pl.BlockSpec(memory_space=pltpu.SMEM)
VMEM = pl.BlockSpec(memory_space=pltpu.VMEM)
PARAMS = pltpu.CompilerParams(vmem_limit_bytes=40 * 2**20)


def words(value):
    high = value.astype(bf16)
    return high, (value - high.astype(f32)).astype(bf16)


def transform_kernel(place, full, mine, other, own, out):
    core = place[0]
    count, rows, nao = mine.shape
    wide = full.shape[1]
    weight = own[...].astype(f32)
    lane = lax.broadcasted_iota(jnp.int32, (1, wide), 1)
    terms = jnp.zeros((1, wide), f32)
    for source, owner in ((mine, core), (other, 1 - core)):
        slab = jnp.dot(
            source[...].reshape(count * rows, nao), full[...], preferred_element_type=f32
        ).astype(bf16)
        for p in range(count):
            block = slab[p * rows : (p + 1) * rows]
            for zb in range(2):
                out[owner * (count // 2) + p // 2, zb, p % 2, 0:rows] = block
            term = jnp.sum(block.astype(f32) * weight, axis=0, keepdims=True)
            term = jnp.sum(term, axis=1, keepdims=True)
            terms += jnp.where(lane == owner * count + p, term, 0.0)
    high, low = words(terms)
    lines = lax.broadcasted_iota(jnp.int32, (16, wide), 0)
    rider = jnp.where(lines == 0, high.astype(f32), jnp.where(lines == 1, low.astype(f32), 0.0))
    rider = rider.astype(bf16)
    for y in range(8):
        for zb in range(2):
            for za in range(2):
                out[y, zb, za, rows : rows + 16] = rider


def exchange_kernel(place, got, got_other, mine, other, out, column_side, row_side):
    core, zb = place[0], place[1]
    count, rows, nao = mine.shape
    wide = got.shape[4]
    half = wide // 2
    for y in range(8):
        for za in range(2):
            for k, source in enumerate((got, got_other)):
                at = pl.ds((2 * y + za) * rows, rows)
                row_side[at, k * wide : (k + 1) * wide] = source[y, zb, za, 0:rows]
                block = source[y, core, za, 0:rows]
                at = pl.ds((4 * y + za) * rows, rows)
                column_side[at, k * wide : (k + 1) * wide] = block
                at = pl.ds((4 * y + 2 + za) * rows, rows)
                column_side[at, k * wide : k * wide + half] = -block[:, half:]
                column_side[at, k * wide + half : (k + 1) * wide] = block[:, :half]

    riders = jnp.zeros((16, wide), f32)
    for y in range(8):
        for b in range(2):
            for za in range(2):
                for source in (got, got_other):
                    riders += source[y, b, za, rows : rows + 16].astype(f32)
    weights = riders[0:1] + riders[1:2]
    lane = lax.broadcasted_iota(jnp.int32, (1, wide), 1)
    for part in range(3):
        at = pl.ds(part * 16, 16)
        total = jnp.zeros((16, nao), f32)
        for source, owner in ((mine, core), (other, 1 - core)):
            for p in range(count):
                weight = jnp.sum(jnp.where(lane == owner * count + p, weights, 0.0), axis=1, keepdims=True)
                total += weight * source[p, at].astype(f32)
        for s in range(8):
            start = s * 4 * rows
            piece = jnp.where(
                core == 0, total[:, start : start + 2 * rows], total[:, start + 2 * rows : start + 4 * rows]
            )
            high, low = words(piece)
            gap = jnp.zeros((16, half - 2 * rows), bf16)
            out[s, 4 * rows : 4 * rows + 16, part * 256 : (part + 1) * 256] = jnp.concatenate(
                [high, gap, low, gap], axis=1
            )

    for n in range(3):
        block = lax.dot_general(
            column_side[...],
            row_side[n * 256 : (n + 1) * 256],
            (((1,), (1,)), ((), ())),
            preferred_element_type=f32,
        ).astype(bf16)
        for s in range(8):
            out[s, 0 : 4 * rows, n * 256 : (n + 1) * 256] = block[s * 4 * rows : (s + 1) * 4 * rows]


def on_device(vectors, coeffs):
    core = lax.axis_index("core")
    zb = lax.axis_index("zb")
    place = jnp.stack([core, zb]).astype(jnp.int32)
    count, rows, nao = vectors.shape
    half = coeffs.shape[2] // 2
    wide = 2 * half
    tall = rows + 16

    other_vectors = lax.ppermute(vectors, "core", SWAP)
    own = lax.dynamic_slice_in_dim(coeffs, core * half, half, 2)
    own = jnp.concatenate([own[0], own[1]], axis=1)
    full = lax.all_to_all(jnp.broadcast_to(own[None], (32, rows, wide)), FAR, 0, 0, tiled=True)

    pieces = pl.pallas_call(
        transform_kernel,
        out_shape=jax.ShapeDtypeStruct((8, 2, 2, tall, wide), bf16),
        in_specs=[SMEM] + [VMEM] * 4,
        out_specs=VMEM,
        compiler_params=PARAMS,
        name="half_transform",
    )(place, full.reshape(nao, wide), vectors, other_vectors, own)
    got = lax.all_to_all(pieces.reshape(32, tall, wide), FAR, 0, 0, tiled=True)
    got_other = lax.ppermute(got, "core", SWAP)

    shape = (8, 2, 2, tall, wide)
    sums = pl.pallas_call(
        exchange_kernel,
        out_shape=jax.ShapeDtypeStruct((8, 4 * rows + 16, 16 * rows), bf16),
        in_specs=[SMEM] + [VMEM] * 4,
        out_specs=VMEM,
        scratch_shapes=[
            pltpu.VMEM((32 * rows, 2 * wide), bf16),
            pltpu.VMEM((16 * rows, 2 * wide), bf16),
        ],
        compiler_params=PARAMS,
        name="exchange_quarter",
    )(place, got.reshape(shape), got_other.reshape(shape), vectors, other_vectors)
    sums = lax.all_to_all(sums, NEAR, 0, 0, tiled=True)
    sums = jnp.sum(sums.astype(f32), axis=0)
    coulomb = sums[4 * rows :].reshape(16, 3, 2, half)[..., : 2 * rows]
    coulomb = (coulomb[:, :, 0] + coulomb[:, :, 1]).transpose(1, 0, 2).reshape(rows, 2 * rows)
    exchange = sums[: 4 * rows].astype(bf16).T.reshape(16, rows, 4 * rows)
    exchange = jnp.sum(lax.all_to_all(exchange, SUMS, 0, 0, tiled=True).astype(f32), axis=0)
    exchange = exchange.reshape(rows, 2, 2 * rows).transpose(1, 0, 2)
    return exchange, coulomb


def solution(mesh):
    fine = Mesh(mesh.devices.reshape(2, 4, 2, 8, 2, 2), ("zl", "x", "core", "y", "zb", "za"))
    chol = ("zl", "x", "core")
    return jax.shard_map(
        on_device,
        mesh=fine,
        in_specs=(P(chol, FAR, None), P(None, FAR, None)),
        out_specs=(P(None, FAR, chol), P(FAR, chol)),
        check_vma=False,
    )
```

```python
import jax
import jax.numpy as jnp
from jax import lax
from jax.experimental import pallas as pl
from jax.experimental.pallas import tpu as pltpu
from jax.sharding import Mesh
from jax.sharding import PartitionSpec as P

NEAR = ("zl", "x")
FAR = ("y", "zb", "za")
SUMS = ("y", "za")
SWAP = [(0, 1), (1, 0)]
f32, bf16 = jnp.float32, jnp.bfloat16
SMEM = pl.BlockSpec(memory_space=pltpu.SMEM)
VMEM = pl.BlockSpec(memory_space=pltpu.VMEM)
PARAMS = pltpu.CompilerParams(vmem_limit_bytes=40 * 2**20)


def words(value):
    high = value.astype(bf16)
    return high, (value - high.astype(f32)).astype(bf16)


def spread_kernel(place, coeffs, own, pieces):
    half = coeffs.shape[2] // 2
    for c in range(2):
        low, high = coeffs[c, :, :half], coeffs[c, :, half:]
        part = jnp.where(place[0] == 0, low.astype(f32), high.astype(f32)).astype(bf16)
        own[:, c * half : (c + 1) * half] = part
        for o in range(pieces.shape[0]):
            pieces[o, :, c * half : (c + 1) * half] = part


def transform_kernel(place, full, mine, other, own, out):
    core = place[0]
    count, rows, nao = mine.shape
    wide = full.shape[1]
    half = wide // 2
    weight = own[...].astype(f32)
    lane = lax.broadcasted_iota(jnp.int32, (1, half), 1)
    terms = jnp.zeros((1, half), f32)
    for source, owner in ((mine, core), (other, 1 - core)):
        slab = jnp.dot(
            source[...].reshape(count * rows, nao), full[...], preferred_element_type=f32
        ).astype(bf16)
        for p in range(count):
            block = slab[p * rows : (p + 1) * rows]
            for zb in range(2):
                out[owner * (count // 2) + p // 2, zb, p % 2, 0:rows] = block[:, :half]
                out[owner * (count // 2) + p // 2, zb, p % 2, rows : 2 * rows] = block[:, half:]
            term = jnp.sum(block.astype(f32) * weight, axis=0, keepdims=True)
            term = jnp.sum(term, axis=1, keepdims=True)
            terms += jnp.where(lane == owner * count + p, term, 0.0)
    high, low = words(terms)
    lines = lax.broadcasted_iota(jnp.int32, (8, half), 0)
    rider = jnp.where(lines == 0, high.astype(f32), jnp.where(lines == 1, low.astype(f32), 0.0))
    rider = rider.astype(bf16)
    for y in range(8):
        for zb in range(2):
            for za in range(2):
                out[y, zb, za, 2 * rows : 2 * rows + 8] = rider


def exchange_kernel(place, got, got_other, mine, other, out, column_side, row_side):
    core, zb = place[0], place[1]
    count, rows, nao = mine.shape
    half = got.shape[4]
    wide = 2 * half
    for y in range(8):
        for za in range(2):
            for k, source in enumerate((got, got_other)):
                left = slice(k * wide, k * wide + half)
                right = slice(k * wide + half, (k + 1) * wide)
                at = pl.ds((2 * y + za) * rows, rows)
                row_side[at, left] = source[y, zb, za, 0:rows]
                row_side[at, right] = source[y, zb, za, rows : 2 * rows]
                real = source[y, core, za, 0:rows]
                imag = source[y, core, za, rows : 2 * rows]
                at = pl.ds((4 * y + za) * rows, rows)
                column_side[at, left] = real
                column_side[at, right] = imag
                at = pl.ds((4 * y + 2 + za) * rows, rows)
                column_side[at, left] = -imag
                column_side[at, right] = real

    riders = jnp.zeros((8, half), f32)
    for y in range(8):
        for b in range(2):
            for za in range(2):
                for source in (got, got_other):
                    riders += source[y, b, za, 2 * rows : 2 * rows + 8].astype(f32)
    weights = riders[0:1] + riders[1:2]
    lane = lax.broadcasted_iota(jnp.int32, (1, half), 1)
    for part in range(3):
        at = pl.ds(part * 16, 16)
        total = jnp.zeros((16, nao), f32)
        for source, owner in ((mine, core), (other, 1 - core)):
            for p in range(count):
                weight = jnp.sum(jnp.where(lane == owner * count + p, weights, 0.0), axis=1, keepdims=True)
                total += weight * source[p, at].astype(f32)
        for s in range(8):
            start = s * 4 * rows
            piece = jnp.where(
                core == 0, total[:, start : start + 2 * rows], total[:, start + 2 * rows : start + 4 * rows]
            )
            high, low = words(piece)
            gap = jnp.zeros((16, half - 2 * rows), bf16)
            out[s, 4 * rows : 4 * rows + 16, part * 256 : (part + 1) * 256] = jnp.concatenate(
                [high, gap, low, gap], axis=1
            )

    for n in range(3):
        block = lax.dot_general(
            column_side[...],
            row_side[n * 256 : (n + 1) * 256],
            (((1,), (1,)), ((), ())),
            preferred_element_type=f32,
        ).astype(bf16)
        for s in range(8):
            out[s, 0 : 4 * rows, n * 256 : (n + 1) * 256] = block[s * 4 * rows : (s + 1) * 4 * rows]


def near_sum_kernel(parts, out, coulomb):
    rows = coulomb.shape[0]
    deep = 4 * rows
    tail = jnp.sum(parts[:, deep : deep + 16].astype(f32), axis=0)
    for part in range(3):
        start = part * 256
        coulomb[part * 16 : (part + 1) * 16] = (
            tail[:, start : start + 2 * rows] + tail[:, start + 128 : start + 128 + 2 * rows]
        )
    for n in range(2):
        columns = slice(n * 8 * rows, (n + 1) * 8 * rows)
        turned = jnp.sum(parts[:, 0:deep, columns].astype(f32), axis=0).T
        for j in range(8):
            block = turned[j * rows : (j + 1) * rows]
            rest = jnp.concatenate([block[: rows // 2, 128:], block[rows // 2 :, 128:]], axis=1)
            out[n * 8 + j, 0:rows] = block[:, :128].astype(bf16)
            out[n * 8 + j, rows : rows + rows // 2] = rest.astype(bf16)


def far_sum_kernel(parts, out):
    rows = out.shape[1]
    total = jnp.sum(parts[...].astype(f32), axis=0)
    rest = jnp.concatenate([total[rows:, :64], total[rows:, 64:]], axis=0)
    out[0] = total[:rows, : 2 * rows]
    out[1] = jnp.concatenate([total[:rows, 2 * rows :], rest], axis=1)


def call(kernel, name, outs, inputs, place=None, scratch=()):
    specs = [VMEM] * len(inputs)
    if place is not None:
        specs, inputs = [SMEM] + specs, (place,) + inputs
    return pl.pallas_call(
        kernel,
        out_shape=[jax.ShapeDtypeStruct(shape, dtype) for shape, dtype in outs],
        in_specs=specs,
        out_specs=[VMEM] * len(outs),
        scratch_shapes=scratch,
        compiler_params=PARAMS,
        name=name,
    )(*inputs)


def on_device(vectors, coeffs):
    core = lax.axis_index("core")
    zb = lax.axis_index("zb")
    place = jnp.stack([core, zb]).astype(jnp.int32)
    count, rows, nao = vectors.shape
    half = coeffs.shape[2] // 2
    wide = 2 * half
    tall = 2 * rows + 8
    deep = 4 * rows + 16

    other_vectors = lax.ppermute(vectors, "core", SWAP)
    own, spread = call(
        spread_kernel, "spread", [((rows, wide), bf16), ((32, rows, wide), bf16)], (coeffs,), place
    )
    full = lax.all_to_all(spread, FAR, 0, 0, tiled=True).reshape(nao, wide)

    shape = (8, 2, 2, tall, half)
    (pieces,) = call(
        transform_kernel, "half_transform", [(shape, bf16)], (full, vectors, other_vectors, own), place
    )
    got = lax.all_to_all(pieces.reshape(32, tall, half), FAR, 0, 0, tiled=True)
    got_other = lax.ppermute(got, "core", SWAP)

    scratch = [pltpu.VMEM((32 * rows, 2 * wide), bf16), pltpu.VMEM((16 * rows, 2 * wide), bf16)]
    (parts,) = call(
        exchange_kernel,
        "exchange_quarter",
        [((8, deep, 16 * rows), bf16)],
        (got.reshape(shape), got_other.reshape(shape), vectors, other_vectors),
        place,
        scratch,
    )
    parts = lax.all_to_all(parts, NEAR, 0, 0, tiled=True)
    packed, coulomb = call(
        near_sum_kernel, "near_sum", [((16, rows + rows // 2, 128), bf16), ((rows, 2 * rows), f32)], (parts,)
    )
    packed = lax.all_to_all(packed, SUMS, 0, 0, tiled=True)
    (exchange,) = call(far_sum_kernel, "far_sum", [((2, rows, 2 * rows), f32)], (packed,))
    return exchange, coulomb


def solution(mesh):
    fine = Mesh(mesh.devices.reshape(2, 4, 2, 8, 2, 2), ("zl", "x", "core", "y", "zb", "za"))
    chol = ("zl", "x", "core")
    return jax.shard_map(
        on_device,
        mesh=fine,
        in_specs=(P(chol, FAR, None), P(None, FAR, None)),
        out_specs=(P(None, FAR, chol), P(FAR, chol)),
        check_vma=False,
    )
```

```python
import jax
import jax.numpy as jnp
from jax import lax
from jax.experimental import pallas as pl
from jax.experimental.pallas import tpu as pltpu
from jax.sharding import Mesh
from jax.sharding import PartitionSpec as P

NEAR = ("zl", "x")
FAR = ("y", "zb", "za")
SUMS = ("y", "za")
SWAP = [(0, 1), (1, 0)]
f32, bf16 = jnp.float32, jnp.bfloat16
SMEM = pl.BlockSpec(memory_space=pltpu.SMEM)
VMEM = pl.BlockSpec(memory_space=pltpu.VMEM)
HBM = pl.BlockSpec(memory_space=pltpu.HBM)
PARAMS = pltpu.CompilerParams(vmem_limit_bytes=40 * 2**20)


def words(value):
    high = value.astype(bf16)
    return high, (value - high.astype(f32)).astype(bf16)


def spread_kernel(place, coeffs, pieces, sems):
    copies = [
        pltpu.make_async_copy(coeffs.at[place[0]], pieces.at[o], sems.at[o]) for o in range(pieces.shape[0])
    ]
    for copy in copies:
        copy.start()
    for copy in copies:
        copy.wait()


def transform_kernel(place, full, mine, other, coeffs, out, held, sem):
    copy = pltpu.make_async_copy(mine, held, sem)
    copy.start()
    core = place[0]
    count, rows, nao = mine.shape
    wide = full.shape[1]
    half = wide // 2
    weight = coeffs[core].astype(f32)
    lane = lax.broadcasted_iota(jnp.int32, (1, half), 1)
    terms = jnp.zeros((1, half), f32)
    for source, owner in ((other, 1 - core), (held, core)):
        if source is held:
            copy.wait()
        slab = jnp.dot(
            source[...].reshape(count * rows, nao), full[...], preferred_element_type=f32
        ).astype(bf16)
        for p in range(count):
            block = slab[p * rows : (p + 1) * rows]
            for zb in range(2):
                out[owner * (count // 2) + p // 2, zb, p % 2, 0:rows] = block[:, :half]
                out[owner * (count // 2) + p // 2, zb, p % 2, rows : 2 * rows] = block[:, half:]
            term = jnp.sum(block.astype(f32) * weight, axis=0, keepdims=True)
            term = jnp.sum(term, axis=1, keepdims=True)
            terms += jnp.where(lane == owner * count + p, term, 0.0)
    high, low = words(terms)
    lines = lax.broadcasted_iota(jnp.int32, (8, half), 0)
    rider = jnp.where(lines == 0, high.astype(f32), jnp.where(lines == 1, low.astype(f32), 0.0))
    rider = rider.astype(bf16)
    for y in range(8):
        for zb in range(2):
            for za in range(2):
                out[y, zb, za, 2 * rows : 2 * rows + 8] = rider


def exchange_kernel(place, got, got_other, mine, other, out, column_side, row_side):
    core, zb = place[0], place[1]
    count, rows, nao = mine.shape
    half = got.shape[4]
    wide = 2 * half
    own_sign = jnp.where(core == 0, 1.0, -1.0).astype(bf16)
    other_sign = jnp.where(core == 0, -1.0, 1.0).astype(bf16)
    for y in range(8):
        for za in range(2):
            for h in range(2):
                own_at = slice(h * half, (h + 1) * half)
                other_at = slice(wide + h * half, wide + (h + 1) * half)
                part = slice(h * rows, (h + 1) * rows)
                at = pl.ds((2 * y + za) * rows, rows)
                row_side[at, own_at] = got[y, zb, za, part]
                row_side[at, other_at] = got_other[y, zb, za, part]
                own = got[y, core, za, part]
                other_part = got_other[y, core, za, part]
                at = pl.ds((4 * y + za) * rows, rows)
                column_side[at, own_at] = own
                column_side[at, other_at] = other_part
                at = pl.ds((4 * y + 2 + za) * rows, rows)
                column_side[at, own_at] = other_part * other_sign
                column_side[at, other_at] = own * own_sign

    riders = jnp.zeros((8, half), f32)
    for y in range(8):
        for b in range(2):
            for za in range(2):
                for source in (got, got_other):
                    riders += source[y, b, za, 2 * rows : 2 * rows + 8].astype(f32)
    weights = riders[0:1] + riders[1:2]
    lane = lax.broadcasted_iota(jnp.int32, (1, half), 1)
    weighted = []
    for source, owner in ((mine, core), (other, 1 - core)):
        for p in range(count):
            weight = jnp.sum(jnp.where(lane == owner * count + p, weights, 0.0), axis=1, keepdims=True)
            weighted.append((source, p, weight))
    for part in range(3):
        at = pl.ds(part * 16, 16)
        total = jnp.zeros((16, nao), f32)
        for source, p, weight in weighted:
            total += weight * source[p, at].astype(f32)
        for s in range(8):
            start = s * 4 * rows
            piece = jnp.where(
                core == 0, total[:, start : start + 2 * rows], total[:, start + 2 * rows : start + 4 * rows]
            )
            high, low = words(piece)
            gap = jnp.zeros((16, half - 2 * rows), bf16)
            out[s, 4 * rows : 4 * rows + 16, part * 256 : (part + 1) * 256] = jnp.concatenate(
                [high, gap, low, gap], axis=1
            )

    for n in range(3):
        block = lax.dot_general(
            column_side[...],
            row_side[n * 256 : (n + 1) * 256],
            (((1,), (1,)), ((), ())),
            preferred_element_type=f32,
        ).astype(bf16)
        for s in range(8):
            out[s, 0 : 4 * rows, n * 256 : (n + 1) * 256] = block[s * 4 * rows : (s + 1) * 4 * rows]


def near_sum_kernel(parts, out, coulomb):
    rows = coulomb.shape[0]
    deep = 4 * rows
    tail = jnp.sum(parts[:, deep : deep + 16].astype(f32), axis=0)
    for part in range(3):
        start = part * 256
        coulomb[part * 16 : (part + 1) * 16] = (
            tail[:, start : start + 2 * rows] + tail[:, start + 128 : start + 128 + 2 * rows]
        )
    for n in range(2):
        columns = slice(n * 8 * rows, (n + 1) * 8 * rows)
        turned = jnp.sum(parts[:, 0:deep, columns].astype(f32), axis=0).T
        for j in range(8):
            block = turned[j * rows : (j + 1) * rows]
            rest = jnp.concatenate([block[: rows // 2, 128:], block[rows // 2 :, 128:]], axis=1)
            out[n * 8 + j, 0:rows] = block[:, :128].astype(bf16)
            out[n * 8 + j, rows : rows + rows // 2] = rest.astype(bf16)


def far_sum_kernel(parts, out):
    rows = out.shape[1]
    total = jnp.sum(parts[...].astype(f32), axis=0)
    rest = jnp.concatenate([total[rows:, :64], total[rows:, 64:]], axis=0)
    out[0] = total[:rows, : 2 * rows]
    out[1] = jnp.concatenate([total[:rows, 2 * rows :], rest], axis=1)


def call(kernel, name, outs, inputs, place=None, scratch=(), specs=None, out_spec=VMEM):
    specs = specs or [VMEM] * len(inputs)
    if place is not None:
        specs, inputs = [SMEM] + specs, (place,) + inputs
    return pl.pallas_call(
        kernel,
        out_shape=[jax.ShapeDtypeStruct(shape, dtype) for shape, dtype in outs],
        in_specs=specs,
        out_specs=[out_spec] * len(outs),
        scratch_shapes=scratch,
        compiler_params=PARAMS,
        name=name,
    )(*inputs)


def on_device(vectors, coeffs):
    core = lax.axis_index("core")
    zb = lax.axis_index("zb")
    place = jnp.stack([core, zb]).astype(jnp.int32)
    count, rows, nao = vectors.shape
    wide = coeffs.shape[2]
    half = wide // 2
    tall = 2 * rows + 8
    deep = 4 * rows + 16

    other_vectors = lax.ppermute(vectors, "core", SWAP)
    (spread,) = call(
        spread_kernel,
        "spread",
        [((32, rows, wide), bf16)],
        (coeffs,),
        place,
        [pltpu.SemaphoreType.DMA((32,))],
        [HBM],
        HBM,
    )
    full = lax.all_to_all(spread, FAR, 0, 0, tiled=True).reshape(nao, wide)

    shape = (8, 2, 2, tall, half)
    (pieces,) = call(
        transform_kernel,
        "half_transform",
        [(shape, bf16)],
        (full, vectors, other_vectors, coeffs),
        place,
        [pltpu.VMEM(vectors.shape, bf16), pltpu.SemaphoreType.DMA],
        [VMEM, HBM, VMEM, VMEM],
    )
    got = lax.all_to_all(pieces.reshape(32, tall, half), FAR, 0, 0, tiled=True)
    got_other = lax.ppermute(got, "core", SWAP)

    scratch = [pltpu.VMEM((32 * rows, 2 * wide), bf16), pltpu.VMEM((16 * rows, 2 * wide), bf16)]
    (parts,) = call(
        exchange_kernel,
        "exchange_quarter",
        [((8, deep, 16 * rows), bf16)],
        (got.reshape(shape), got_other.reshape(shape), vectors, other_vectors),
        place,
        scratch,
    )
    parts = lax.all_to_all(parts, NEAR, 0, 0, tiled=True)
    packed, coulomb = call(
        near_sum_kernel, "near_sum", [((16, rows + rows // 2, 128), bf16), ((rows, 2 * rows), f32)], (parts,)
    )
    packed = lax.all_to_all(packed, SUMS, 0, 0, tiled=True)
    (exchange,) = call(far_sum_kernel, "far_sum", [((2, rows, 2 * rows), f32)], (packed,))
    return exchange, coulomb


def solution(mesh):
    fine = Mesh(mesh.devices.reshape(2, 4, 2, 8, 2, 2), ("zl", "x", "core", "y", "zb", "za"))
    chol = ("zl", "x", "core")
    return jax.shard_map(
        on_device,
        mesh=fine,
        in_specs=(P(chol, FAR, None), P(None, FAR, None)),
        out_specs=(P(None, FAR, chol), P(FAR, chol)),
        check_vma=False,
    )
```

```python
import jax
import jax.numpy as jnp
from jax import lax
from jax.experimental import pallas as pl
from jax.experimental.pallas import tpu as pltpu
from jax.sharding import Mesh
from jax.sharding import PartitionSpec as P

NEAR = ("zl", "x")
FAR = ("y", "zb", "za")
SUMS = ("y", "za")
SWAP = [(0, 1), (1, 0)]
f32, bf16 = jnp.float32, jnp.bfloat16
SMEM = pl.BlockSpec(memory_space=pltpu.SMEM)
VMEM = pl.BlockSpec(memory_space=pltpu.VMEM)


def words(value):
    high = value.astype(bf16)
    return high, (value - high.astype(f32)).astype(bf16)


def transform_kernel(place, full, mine, other, own, out):
    core = place[0]
    count, rows, nao = mine.shape
    wide = full.shape[1]
    half = wide // 2
    weight = own[...].astype(f32)
    lane = lax.broadcasted_iota(jnp.int32, (1, half), 1)
    terms = jnp.zeros((1, half), f32)
    for source, owner in ((mine, core), (other, 1 - core)):
        slab = jnp.dot(
            source[...].reshape(count * rows, nao), full[...], preferred_element_type=f32
        ).astype(bf16)
        for p in range(count):
            block = slab[p * rows : (p + 1) * rows]
            for zb in range(2):
                out[owner * (count // 2) + p // 2, zb, p % 2, 0:rows] = block[:, :half]
                out[owner * (count // 2) + p // 2, zb, p % 2, rows : 2 * rows] = block[:, half:]
            term = jnp.sum(block.astype(f32) * weight, axis=0, keepdims=True)
            term = jnp.sum(term, axis=1, keepdims=True)
            terms += jnp.where(lane == owner * count + p, term, 0.0)
    high, low = words(terms)
    lines = lax.broadcasted_iota(jnp.int32, (8, half), 0)
    rider = jnp.where(lines == 0, high.astype(f32), jnp.where(lines == 1, low.astype(f32), 0.0))
    rider = rider.astype(bf16)
    for y in range(8):
        for zb in range(2):
            for za in range(2):
                out[y, zb, za, 2 * rows : 2 * rows + 8] = rider


def exchange_kernel(place, got, got_other, mine, other, out, column_side, row_side):
    core, zb = place[0], place[1]
    count, rows, nao = mine.shape
    half = got.shape[4]
    wide = 2 * half
    own_sign = jnp.where(core == 0, 1.0, -1.0).astype(bf16)
    other_sign = jnp.where(core == 0, -1.0, 1.0).astype(bf16)
    for y in range(8):
        for za in range(2):
            for h in range(2):
                own_at = slice(h * half, (h + 1) * half)
                other_at = slice(wide + h * half, wide + (h + 1) * half)
                part = slice(h * rows, (h + 1) * rows)
                at = pl.ds((2 * y + za) * rows, rows)
                row_side[at, own_at] = got[y, zb, za, part]
                row_side[at, other_at] = got_other[y, zb, za, part]
                own = got[y, core, za, part]
                other_part = got_other[y, core, za, part]
                at = pl.ds((4 * y + za) * rows, rows)
                column_side[at, own_at] = own
                column_side[at, other_at] = other_part
                at = pl.ds((4 * y + 2 + za) * rows, rows)
                column_side[at, own_at] = other_part * other_sign
                column_side[at, other_at] = own * own_sign

    riders = jnp.zeros((8, half), f32)
    for y in range(8):
        for b in range(2):
            for za in range(2):
                for source in (got, got_other):
                    riders += source[y, b, za, 2 * rows : 2 * rows + 8].astype(f32)
    weights = riders[0:1] + riders[1:2]
    lane = lax.broadcasted_iota(jnp.int32, (1, half), 1)
    weighted = []
    for source, owner in ((mine, core), (other, 1 - core)):
        for p in range(count):
            weight = jnp.sum(jnp.where(lane == owner * count + p, weights, 0.0), axis=1, keepdims=True)
            weighted.append((source, p, weight))
    for part in range(3):
        at = pl.ds(part * 16, 16)
        total = jnp.zeros((16, nao), f32)
        for source, p, weight in weighted:
            total += weight * source[p, at].astype(f32)
        for s in range(8):
            start = s * 4 * rows
            piece = jnp.where(
                core == 0, total[:, start : start + 2 * rows], total[:, start + 2 * rows : start + 4 * rows]
            )
            high, low = words(piece)
            gap = jnp.zeros((16, half - 2 * rows), bf16)
            out[s, 4 * rows : 4 * rows + 16, part * 256 : (part + 1) * 256] = jnp.concatenate(
                [high, gap, low, gap], axis=1
            )

    for n in range(3):
        block = lax.dot_general(
            column_side[...],
            row_side[n * 256 : (n + 1) * 256],
            (((1,), (1,)), ((), ())),
            preferred_element_type=f32,
        ).astype(bf16)
        for s in range(8):
            out[s, 0 : 4 * rows, n * 256 : (n + 1) * 256] = block[s * 4 * rows : (s + 1) * 4 * rows]


def near_sum_kernel(parts, out, coulomb):
    rows = coulomb.shape[0]
    deep = 4 * rows
    tail = jnp.sum(parts[:, deep : deep + 16].astype(f32), axis=0)
    for part in range(3):
        start = part * 256
        coulomb[part * 16 : (part + 1) * 16] = (
            tail[:, start : start + 2 * rows] + tail[:, start + 128 : start + 128 + 2 * rows]
        )
    for n in range(2):
        columns = slice(n * 8 * rows, (n + 1) * 8 * rows)
        turned = jnp.sum(parts[:, 0:deep, columns].astype(f32), axis=0).T
        for j in range(8):
            block = turned[j * rows : (j + 1) * rows]
            rest = jnp.concatenate([block[: rows // 2, 128:], block[rows // 2 :, 128:]], axis=1)
            out[n * 8 + j, 0:rows] = block[:, :128].astype(bf16)
            out[n * 8 + j, rows : rows + rows // 2] = rest.astype(bf16)


def far_sum_kernel(parts, out):
    rows = out.shape[1]
    total = jnp.sum(parts[...].astype(f32), axis=0)
    rest = jnp.concatenate([total[rows:, :64], total[rows:, 64:]], axis=0)
    out[0] = total[:rows, : 2 * rows]
    out[1] = jnp.concatenate([total[:rows, 2 * rows :], rest], axis=1)


def call(kernel, name, grant, outs, inputs, place=None, scratch=()):
    specs = [VMEM] * len(inputs)
    if place is not None:
        specs, inputs = [SMEM] + specs, (place,) + inputs
    return pl.pallas_call(
        kernel,
        out_shape=[jax.ShapeDtypeStruct(shape, dtype) for shape, dtype in outs],
        in_specs=specs,
        out_specs=[VMEM] * len(outs),
        scratch_shapes=scratch,
        compiler_params=pltpu.CompilerParams(vmem_limit_bytes=grant * 2**20),
        name=name,
    )(*inputs)


def on_device(vectors, coeffs):
    core = lax.axis_index("core")
    zb = lax.axis_index("zb")
    place = jnp.stack([core, zb]).astype(jnp.int32)
    count, rows, nao = vectors.shape
    wide = coeffs.shape[2]
    half = wide // 2
    tall = 2 * rows + 8
    deep = 4 * rows + 16

    other_vectors = lax.ppermute(vectors, "core", SWAP)
    own = lax.dynamic_index_in_dim(coeffs, core, 0, keepdims=False)
    full = lax.all_to_all(jnp.broadcast_to(own[None], (32, rows, wide)), FAR, 0, 0, tiled=True).reshape(nao, wide)

    shape = (8, 2, 2, tall, half)
    (pieces,) = call(
        transform_kernel,
        "half_transform",
        16,
        [(shape, bf16)],
        (full, vectors, other_vectors, own),
        place,
    )
    got = lax.all_to_all(pieces.reshape(32, tall, half), FAR, 0, 0, tiled=True)
    got_other = lax.ppermute(got, "core", SWAP)

    scratch = [pltpu.VMEM((32 * rows, 2 * wide), bf16), pltpu.VMEM((16 * rows, 2 * wide), bf16)]
    (parts,) = call(
        exchange_kernel,
        "exchange_quarter",
        24,
        [((8, deep, 16 * rows), bf16)],
        (got.reshape(shape), got_other.reshape(shape), vectors, other_vectors),
        place,
        scratch,
    )
    parts = lax.all_to_all(parts, NEAR, 0, 0, tiled=True)
    packed, coulomb = call(
        near_sum_kernel, "near_sum", 12, [((16, rows + rows // 2, 128), bf16), ((rows, 2 * rows), f32)], (parts,)
    )
    packed = lax.all_to_all(packed, SUMS, 0, 0, tiled=True)
    (exchange,) = call(far_sum_kernel, "far_sum", 4, [((2, rows, 2 * rows), f32)], (packed,))
    return exchange, coulomb


def solution(mesh):
    fine = Mesh(mesh.devices.reshape(2, 4, 2, 8, 2, 2), ("zl", "x", "core", "y", "zb", "za"))
    chol = ("zl", "x", "core")
    return jax.shard_map(
        on_device,
        mesh=fine,
        in_specs=(P(chol, FAR, None), P(None, FAR, None)),
        out_specs=(P(None, FAR, chol), P(FAR, chol)),
        check_vma=False,
    )
```

```python
import jax
import jax.numpy as jnp
from jax import lax
from jax.experimental import pallas as pl
from jax.experimental.pallas import tpu as pltpu
from jax.sharding import Mesh
from jax.sharding import PartitionSpec as P

NEAR = ("zl", "x")
FAR = ("y", "zb", "za")
SUMS = ("y", "za")
SWAP = [(0, 1), (1, 0)]
f32, bf16 = jnp.float32, jnp.bfloat16
SMEM = pl.BlockSpec(memory_space=pltpu.SMEM)
VMEM = pl.BlockSpec(memory_space=pltpu.VMEM)
ANY = pl.BlockSpec(memory_space=pl.ANY)


def words(value):
    high = value.astype(bf16)
    return high, (value - high.astype(f32)).astype(bf16)


def transform_kernel(place, full, mine, other, coeffs, out):
    core = place[0]
    count, rows, nao = mine.shape
    wide = full.shape[1]
    half = wide // 2
    weight = coeffs[core].astype(f32)
    lane = lax.broadcasted_iota(jnp.int32, (1, half), 1)
    terms = jnp.zeros((1, half), f32)
    for source, owner in ((mine, core), (other, 1 - core)):
        slab = jnp.dot(
            source[...].reshape(count * rows, nao), full[...], preferred_element_type=f32
        ).astype(bf16)
        for p in range(count):
            block = slab[p * rows : (p + 1) * rows]
            for zb in range(2):
                out[owner * (count // 2) + p // 2, zb, p % 2, 0:rows] = block[:, :half]
                out[owner * (count // 2) + p // 2, zb, p % 2, rows : 2 * rows] = block[:, half:]
            term = jnp.sum(block.astype(f32) * weight, axis=0, keepdims=True)
            term = jnp.sum(term, axis=1, keepdims=True)
            terms += jnp.where(lane == owner * count + p, term, 0.0)
    high, low = words(terms)
    lines = lax.broadcasted_iota(jnp.int32, (8, half), 0)
    rider = jnp.where(lines == 0, high.astype(f32), jnp.where(lines == 1, low.astype(f32), 0.0))
    rider = rider.astype(bf16)
    for y in range(8):
        for zb in range(2):
            for za in range(2):
                out[y, zb, za, 2 * rows : 2 * rows + 8] = rider


def exchange_kernel(place, got, got_other, out, column_side, row_side):
    core, zb = place[0], place[1]
    half = got.shape[4]
    rows = got.shape[3] // 2 // 16 * 16
    wide = 2 * half
    own_sign = jnp.where(core == 0, 1.0, -1.0).astype(bf16)
    other_sign = jnp.where(core == 0, -1.0, 1.0).astype(bf16)
    for y in range(8):
        for za in range(2):
            for h in range(2):
                own_at = slice(h * half, (h + 1) * half)
                other_at = slice(wide + h * half, wide + (h + 1) * half)
                part = slice(h * rows, (h + 1) * rows)
                at = pl.ds((2 * y + za) * rows, rows)
                row_side[at, own_at] = got[y, zb, za, part]
                row_side[at, other_at] = got_other[y, zb, za, part]
                own = got[y, core, za, part]
                other_part = got_other[y, core, za, part]
                at = pl.ds((4 * y + za) * rows, rows)
                column_side[at, own_at] = own
                column_side[at, other_at] = other_part
                at = pl.ds((4 * y + 2 + za) * rows, rows)
                column_side[at, own_at] = other_part * other_sign
                column_side[at, other_at] = own * own_sign

    for n in range(3):
        block = lax.dot_general(
            column_side[...],
            row_side[n * 256 : (n + 1) * 256],
            (((1,), (1,)), ((), ())),
            preferred_element_type=f32,
        ).astype(bf16)
        for s in range(8):
            out[s, 0 : 4 * rows, n * 256 : (n + 1) * 256] = block[s * 4 * rows : (s + 1) * 4 * rows]


def coulomb_kernel(place, got, got_other, mine, other, after, out):
    del after
    core = place[0]
    count, rows, nao = mine.shape
    half = got.shape[4]
    riders = jnp.zeros((8, half), f32)
    for y in range(8):
        for b in range(2):
            for za in range(2):
                for source in (got, got_other):
                    riders += source[y, b, za, 2 * rows : 2 * rows + 8].astype(f32)
    weights = riders[0:1] + riders[1:2]
    lane = lax.broadcasted_iota(jnp.int32, (1, half), 1)
    weighted = []
    for source, owner in ((mine, core), (other, 1 - core)):
        for p in range(count):
            weight = jnp.sum(jnp.where(lane == owner * count + p, weights, 0.0), axis=1, keepdims=True)
            weighted.append((source, p, weight))
    for part in range(3):
        at = pl.ds(part * 16, 16)
        total = jnp.zeros((16, nao), f32)
        for source, p, weight in weighted:
            total += weight * source[p, at].astype(f32)
        for s in range(8):
            start = s * 4 * rows
            out[s, at] = jnp.where(
                core == 0, total[:, start : start + 2 * rows], total[:, start + 2 * rows : start + 4 * rows]
            )


def near_sum_kernel(parts, out):
    rows = parts.shape[1] // 4
    for n in range(2):
        columns = slice(n * 8 * rows, (n + 1) * 8 * rows)
        turned = jnp.sum(parts[:, :, columns].astype(f32), axis=0).T
        for j in range(8):
            block = turned[j * rows : (j + 1) * rows]
            rest = jnp.concatenate([block[: rows // 2, 128:], block[rows // 2 :, 128:]], axis=1)
            out[n * 8 + j, 0:rows] = block[:, :128].astype(bf16)
            out[n * 8 + j, rows : rows + rows // 2] = rest.astype(bf16)


def far_sum_kernel(parts, out):
    rows = out.shape[1]
    total = jnp.sum(parts[...].astype(f32), axis=0)
    rest = jnp.concatenate([total[rows:, :64], total[rows:, 64:]], axis=0)
    out[0] = total[:rows, : 2 * rows]
    out[1] = jnp.concatenate([total[:rows, 2 * rows :], rest], axis=1)


def call(kernel, name, grant, outs, inputs, place=None, scratch=(), specs=None):
    specs = specs or [VMEM] * len(inputs)
    if place is not None:
        specs, inputs = [SMEM] + specs, (place,) + inputs
    return pl.pallas_call(
        kernel,
        out_shape=[jax.ShapeDtypeStruct(shape, dtype) for shape, dtype in outs],
        in_specs=specs,
        out_specs=[VMEM] * len(outs),
        scratch_shapes=scratch,
        compiler_params=pltpu.CompilerParams(vmem_limit_bytes=grant * 2**20),
        name=name,
    )(*inputs)


def near_sum(terms):
    x = lax.axis_index("x")
    zl = lax.axis_index("zl")

    def pick(block, index, axis):
        return lax.dynamic_index_in_dim(block, index, axis, keepdims=False)

    for step, axis in ((1, 2), (2, 1)):
        bit = x // step % 2
        sent = lax.ppermute(pick(terms, 1 - bit, axis), "x", [(i, i ^ step) for i in range(4)])
        terms = pick(terms, bit, axis) + sent
    return pick(terms, zl, 0) + lax.ppermute(pick(terms, 1 - zl, 0), "zl", SWAP)


def on_device(vectors, coeffs):
    core = lax.axis_index("core")
    zb = lax.axis_index("zb")
    place = jnp.stack([core, zb]).astype(jnp.int32)
    count, rows, nao = vectors.shape
    wide = coeffs.shape[2]
    half = wide // 2
    tall = 2 * rows + 8

    other_vectors = lax.ppermute(vectors, "core", SWAP)
    spread = jnp.broadcast_to(lax.dynamic_index_in_dim(coeffs, core, 0), (32, rows, wide))
    full = lax.all_to_all(spread, FAR, 0, 0, tiled=True).reshape(nao, wide)

    shape = (8, 2, 2, tall, half)
    (pieces,) = call(
        transform_kernel,
        "half_transform",
        16,
        [(shape, bf16)],
        (full, vectors, other_vectors, coeffs),
        place,
    )
    got = lax.all_to_all(pieces.reshape(32, tall, half), FAR, 0, 0, tiled=True)
    got_other = lax.ppermute(got, "core", SWAP)

    scratch = [pltpu.VMEM((32 * rows, 2 * wide), bf16), pltpu.VMEM((16 * rows, 2 * wide), bf16)]
    (parts,) = call(
        exchange_kernel,
        "exchange_quarter",
        24,
        [((8, 4 * rows, 16 * rows), bf16)],
        (got.reshape(shape), got_other.reshape(shape)),
        place,
        scratch,
    )
    (terms,) = call(
        coulomb_kernel,
        "coulomb",
        12,
        [((8, rows, 2 * rows), f32)],
        (got.reshape(shape), got_other.reshape(shape), vectors, other_vectors, parts),
        place,
        specs=[VMEM] * 4 + [ANY],
    )
    coulomb = near_sum(terms.reshape(2, 2, 2, rows, 2 * rows))
    parts = lax.all_to_all(parts, NEAR, 0, 0, tiled=True)
    (packed,) = call(near_sum_kernel, "near_sum", 12, [((16, rows + rows // 2, 128), bf16)], (parts,))
    packed = lax.all_to_all(packed, SUMS, 0, 0, tiled=True)
    (exchange,) = call(far_sum_kernel, "far_sum", 4, [((2, rows, 2 * rows), f32)], (packed,))
    return exchange, coulomb


def solution(mesh):
    fine = Mesh(mesh.devices.reshape(2, 4, 2, 8, 2, 2), ("zl", "x", "core", "y", "zb", "za"))
    chol = ("zl", "x", "core")
    return jax.shard_map(
        on_device,
        mesh=fine,
        in_specs=(P(chol, FAR, None), P(None, FAR, None)),
        out_specs=(P(None, FAR, chol), P(FAR, chol)),
        check_vma=False,
    )
```

```python
import jax
import jax.numpy as jnp
from jax import lax
from jax.experimental import pallas as pl
from jax.experimental.pallas import tpu as pltpu
from jax.sharding import Mesh
from jax.sharding import PartitionSpec as P

NEAR = ("zl", "x")
FAR = ("y", "zb", "za")
SUMS = ("y",)
SWAP = [(0, 1), (1, 0)]
f32, bf16 = jnp.float32, jnp.bfloat16
SMEM = pl.BlockSpec(memory_space=pltpu.SMEM)
VMEM = pl.BlockSpec(memory_space=pltpu.VMEM)


def words(value):
    high = value.astype(bf16)
    return high, (value - high.astype(f32)).astype(bf16)


def coulomb_place(word):
    return word // 3 * 16, word % 3 * 128


def transform_kernel(place, full, mine, other, own, out):
    core = place[0]
    count, rows, nao = mine.shape
    wide = full.shape[1]
    half = wide // 2
    weight = own[...].astype(f32)
    lane = lax.broadcasted_iota(jnp.int32, (1, half), 1)
    terms = jnp.zeros((1, half), f32)
    for source, owner in ((mine, core), (other, 1 - core)):
        slab = jnp.dot(
            source[...].reshape(count * rows, nao), full[...], preferred_element_type=f32
        ).astype(bf16)
        for p in range(count):
            block = slab[p * rows : (p + 1) * rows]
            for z in range(4):
                for h in range(2):
                    at = pl.ds((p % 2 * 2 + h) * rows, rows)
                    out[owner * (count // 2) + p // 2, z, at] = block[:, h * half : (h + 1) * half]
            term = jnp.sum(block.astype(f32) * weight, axis=0, keepdims=True)
            term = jnp.sum(term, axis=1, keepdims=True)
            terms += jnp.where(lane == owner * count + p, term, 0.0)
    high, low = words(terms)
    lines = lax.broadcasted_iota(jnp.int32, (8, half), 0)
    rider = jnp.where(lines == 0, high.astype(f32), jnp.where(lines == 1, low.astype(f32), 0.0))
    rider = rider.astype(bf16)
    for y in range(8):
        for z in range(4):
            out[y, z, 4 * rows : 4 * rows + 8] = rider


def exchange_kernel(place, got, got_other, mine, other, out, column_side, row_side):
    core, z = place[0], place[1]
    count, rows, nao = mine.shape
    half = got.shape[3]
    wide = 4 * half
    own_sign = jnp.where(core == 0, 1.0, -1.0).astype(bf16)
    other_sign = jnp.where(core == 0, -1.0, 1.0).astype(bf16)
    for y in range(8):
        for h in range(4):
            own_at = slice(h * half, (h + 1) * half)
            other_at = slice(wide + h * half, wide + (h + 1) * half)
            part = slice(h * rows, (h + 1) * rows)
            at = pl.ds(y * rows, rows)
            row_side[at, own_at] = got[y, z, part]
            row_side[at, other_at] = got_other[y, z, part]
            for za in range(2):
                own = got[y, 2 * core + za, part]
                other_part = got_other[y, 2 * core + za, part]
                at = pl.ds((4 * y + za) * rows, rows)
                column_side[at, own_at] = own
                column_side[at, other_at] = other_part
                at = pl.ds((4 * y + 2 + za) * rows, rows)
                column_side[at, own_at] = other_part * other_sign
                column_side[at, other_at] = own * own_sign

    riders = jnp.zeros((8, half), f32)
    for y in range(8):
        for b in range(4):
            for source in (got, got_other):
                riders += source[y, b, 4 * rows : 4 * rows + 8].astype(f32)
    weights = riders[0:1] + riders[1:2]
    lane = lax.broadcasted_iota(jnp.int32, (1, half), 1)
    weighted = []
    for source, owner in ((mine, core), (other, 1 - core)):
        for p in range(count):
            weight = jnp.sum(jnp.where(lane == owner * count + p, weights, 0.0), axis=1, keepdims=True)
            weighted.append((source, p, weight))
    for part in range(3):
        at = pl.ds(part * 16, 16)
        total = jnp.zeros((16, nao), f32)
        for source, p, weight in weighted:
            total += weight * source[p, at].astype(f32)
        for s in range(8):
            start = s * 4 * rows
            piece = jnp.where(
                core == 0, total[:, start : start + 2 * rows], total[:, start + 2 * rows : start + 4 * rows]
            )
            high, low = words(piece)
            gap = jnp.zeros((16, half - 2 * rows), bf16)
            for k, word in enumerate((high, low)):
                row, column = coulomb_place(2 * part + k)
                at_row = pl.ds(4 * rows + row, 16)
                out[s, at_row, column : column + half] = jnp.concatenate([word, gap], axis=1)

    for n in range(2):
        m = slice(n * 16 * rows, (n + 1) * 16 * rows)
        block = lax.dot_general(
            column_side[m], row_side[...], (((1,), (1,)), ((), ())), preferred_element_type=f32
        ).astype(bf16)
        for s in range(4):
            out[n * 4 + s, 0 : 4 * rows] = block[s * 4 * rows : (s + 1) * 4 * rows]


def near_sum_kernel(parts, out, coulomb):
    rows = coulomb.shape[0]
    deep = 4 * rows
    tail = jnp.sum(parts[:, deep : deep + 32].astype(f32), axis=0)
    for part in range(3):
        total = jnp.zeros((16, 2 * rows), f32)
        for k in range(2):
            row, column = coulomb_place(2 * part + k)
            total += tail[row : row + 16, column : column + 2 * rows]
        coulomb[part * 16 : (part + 1) * 16] = total
    turned = jnp.sum(parts[:, 0:deep].astype(f32), axis=0).T
    for j in range(8):
        block = turned[j * rows : (j + 1) * rows]
        rest = jnp.concatenate([block[: rows // 2, 128:], block[rows // 2 :, 128:]], axis=1)
        out[j, 0:rows] = block[:, :128].astype(bf16)
        out[j, rows : rows + rows // 2] = rest.astype(bf16)


def far_sum_kernel(parts, out):
    rows = out.shape[1]
    total = jnp.sum(parts[...].astype(f32), axis=0)
    rest = jnp.concatenate([total[rows:, :64], total[rows:, 64:]], axis=0)
    out[0] = total[:rows, : 2 * rows]
    out[1] = jnp.concatenate([total[:rows, 2 * rows :], rest], axis=1)


def call(kernel, name, grant, outs, inputs, place=None, scratch=()):
    specs = [VMEM] * len(inputs)
    if place is not None:
        specs, inputs = [SMEM] + specs, (place,) + inputs
    return pl.pallas_call(
        kernel,
        out_shape=[jax.ShapeDtypeStruct(shape, dtype) for shape, dtype in outs],
        in_specs=specs,
        out_specs=[VMEM] * len(outs),
        scratch_shapes=scratch,
        compiler_params=pltpu.CompilerParams(vmem_limit_bytes=grant * 2**20),
        name=name,
    )(*inputs)


def on_device(vectors, coeffs):
    core = lax.axis_index("core")
    z = lax.axis_index("zb") * 2 + lax.axis_index("za")
    place = jnp.stack([core, z]).astype(jnp.int32)
    count, rows, nao = vectors.shape
    wide = coeffs.shape[2]
    half = wide // 2
    tall = 4 * rows + 8
    deep = 4 * rows + 32

    other_vectors = lax.ppermute(vectors, "core", SWAP)
    own = lax.dynamic_index_in_dim(coeffs, core, 0, keepdims=False)
    full = lax.all_to_all(jnp.broadcast_to(own[None], (32, rows, wide)), FAR, 0, 0, tiled=True).reshape(nao, wide)

    shape = (8, 4, tall, half)
    (pieces,) = call(
        transform_kernel,
        "half_transform",
        16,
        [(shape, bf16)],
        (full, vectors, other_vectors, own),
        place,
    )
    got = lax.all_to_all(pieces.reshape(32, tall, half), FAR, 0, 0, tiled=True)
    got_other = lax.ppermute(got, "core", SWAP)

    scratch = [pltpu.VMEM((32 * rows, 4 * wide), bf16), pltpu.VMEM((8 * rows, 4 * wide), bf16)]
    (parts,) = call(
        exchange_kernel,
        "exchange_part",
        28,
        [((8, deep, 8 * rows), bf16)],
        (got.reshape(shape), got_other.reshape(shape), vectors, other_vectors),
        place,
        scratch,
    )
    parts = lax.all_to_all(parts, NEAR, 0, 0, tiled=True)
    packed, coulomb = call(
        near_sum_kernel, "near_sum", 12, [((8, rows + rows // 2, 128), bf16), ((rows, 2 * rows), f32)], (parts,)
    )
    packed = lax.all_to_all(packed, SUMS, 0, 0, tiled=True)
    (exchange,) = call(far_sum_kernel, "far_sum", 4, [((2, rows, 2 * rows), f32)], (packed,))
    return exchange, coulomb


def solution(mesh):
    fine = Mesh(mesh.devices.reshape(2, 4, 2, 8, 2, 2), ("zl", "x", "core", "y", "zb", "za"))
    chol = ("zl", "x", "core")
    return jax.shard_map(
        on_device,
        mesh=fine,
        in_specs=(P(chol, FAR, None), P(None, FAR, None)),
        out_specs=(P(None, FAR, chol), P(FAR, chol)),
        check_vma=False,
    )
```

```python
import jax
import jax.numpy as jnp
from jax import lax
from jax.experimental import pallas as pl
from jax.experimental.pallas import tpu as pltpu
from jax.sharding import Mesh
from jax.sharding import PartitionSpec as P

NEAR = ("zl", "x")
FAR = ("y", "zb", "za")
SUMS = ("y", "za")
SWAP = [(0, 1), (1, 0)]
f32, bf16 = jnp.float32, jnp.bfloat16
VMEM = pl.BlockSpec(memory_space=pltpu.VMEM)


def words(value):
    high = value.astype(bf16)
    return high, (value - high.astype(f32)).astype(bf16)


def vector_lanes(core, count, width):
    row = lax.broadcasted_iota(jnp.int32, (2 * count, width), 0)
    lane = lax.broadcasted_iota(jnp.int32, (2 * count, width), 1)
    return lane == jnp.where(core == 0, row, jnp.where(row < count, row + count, row - count))


def transform_kernel(full, mine, other, own, out):
    core = lax.axis_index("core")
    count, rows, nao = mine.shape
    wide = full.shape[1]
    half = wide // 2
    weight = own[...].astype(f32)
    terms = []
    for source, owner in ((mine, core), (other, 1 - core)):
        slab = jnp.dot(
            source[...].reshape(count * rows, nao), full[...], preferred_element_type=f32
        ).astype(bf16)
        for p in range(count):
            block = slab[p * rows : (p + 1) * rows]
            for zb in range(2):
                out[owner * (count // 2) + p // 2, zb, p % 2, 0:rows] = block[:, :half]
                out[owner * (count // 2) + p // 2, zb, p % 2, rows : 2 * rows] = block[:, half:]
            terms.append(jnp.sum(block.astype(f32) * weight, axis=0, keepdims=True))
    terms = jnp.sum(jnp.concatenate(terms), axis=1, keepdims=True)
    high, low = words(jnp.sum(jnp.where(vector_lanes(core, count, half), terms, 0.0), axis=0, keepdims=True))
    lines = lax.broadcasted_iota(jnp.int32, (8, half), 0)
    rider = jnp.where(lines == 0, high.astype(f32), jnp.where(lines == 1, low.astype(f32), 0.0))
    rider = rider.astype(bf16)
    for y in range(8):
        for zb in range(2):
            for za in range(2):
                out[y, zb, za, 2 * rows : 2 * rows + 8] = rider


def exchange_kernel(got, got_other, mine, other, out, column_side, row_side):
    core, zb = lax.axis_index("core"), lax.axis_index("zb")
    count, rows, nao = mine.shape
    half = got.shape[4]
    wide = 2 * half
    own_sign = jnp.where(core == 0, 1.0, -1.0).astype(bf16)
    other_sign = jnp.where(core == 0, -1.0, 1.0).astype(bf16)
    for y in range(8):
        for za in range(2):
            for h in range(2):
                own_at = slice(h * half, (h + 1) * half)
                other_at = slice(wide + h * half, wide + (h + 1) * half)
                part = slice(h * rows, (h + 1) * rows)
                at = pl.ds((2 * y + za) * rows, rows)
                row_side[at, own_at] = got[y, zb, za, part]
                row_side[at, other_at] = got_other[y, zb, za, part]
                own = got[y, core, za, part]
                other_part = got_other[y, core, za, part]
                at = pl.ds((4 * y + za) * rows, rows)
                column_side[at, own_at] = own
                column_side[at, other_at] = other_part
                at = pl.ds((4 * y + 2 + za) * rows, rows)
                column_side[at, own_at] = other_part * other_sign
                column_side[at, other_at] = own * own_sign

    riders = jnp.zeros((8, half), f32)
    for y in range(8):
        for b in range(2):
            for za in range(2):
                for source in (got, got_other):
                    riders += source[y, b, za, 2 * rows : 2 * rows + 8].astype(f32)
    weights = riders[0:1] + riders[1:2]
    weights = jnp.sum(jnp.where(vector_lanes(core, count, half), weights, 0.0), axis=1, keepdims=True)
    for part in range(3):
        at = pl.ds(part * 16, 16)
        total = jnp.zeros((16, nao), f32)
        for k, source in enumerate((mine, other)):
            for p in range(count):
                total += weights[k * count + p : k * count + p + 1] * source[p, at].astype(f32)
        for s in range(8):
            start = s * 4 * rows
            piece = jnp.where(
                core == 0, total[:, start : start + 2 * rows], total[:, start + 2 * rows : start + 4 * rows]
            )
            high, low = words(piece)
            gap = jnp.zeros((16, half - 2 * rows), bf16)
            out[s, 4 * rows : 4 * rows + 16, part * 256 : (part + 1) * 256] = jnp.concatenate(
                [high, gap, low, gap], axis=1
            )

    for n in range(3):
        block = lax.dot_general(
            column_side[...],
            row_side[n * 256 : (n + 1) * 256],
            (((1,), (1,)), ((), ())),
            preferred_element_type=f32,
        ).astype(bf16)
        for s in range(8):
            out[s, 0 : 4 * rows, n * 256 : (n + 1) * 256] = block[s * 4 * rows : (s + 1) * 4 * rows]


def near_sum_kernel(parts, out, coulomb):
    rows = coulomb.shape[0]
    deep = 4 * rows
    tail = jnp.sum(parts[:, deep : deep + 16].astype(f32), axis=0)
    for part in range(3):
        start = part * 256
        coulomb[part * 16 : (part + 1) * 16] = (
            tail[:, start : start + 2 * rows] + tail[:, start + 128 : start + 128 + 2 * rows]
        )
    for n in range(2):
        columns = slice(n * 8 * rows, (n + 1) * 8 * rows)
        turned = jnp.sum(parts[:, 0:deep, columns].astype(f32), axis=0).T
        for j in range(8):
            block = turned[j * rows : (j + 1) * rows]
            rest = jnp.concatenate([block[: rows // 2, 128:], block[rows // 2 :, 128:]], axis=1)
            out[n * 8 + j, 0:rows] = block[:, :128].astype(bf16)
            out[n * 8 + j, rows : rows + rows // 2] = rest.astype(bf16)


def far_sum_kernel(parts, out):
    rows = out.shape[1]
    total = jnp.sum(parts[...].astype(f32), axis=0)
    rest = jnp.concatenate([total[rows:, :64], total[rows:, 64:]], axis=0)
    out[0] = total[:rows, : 2 * rows]
    out[1] = jnp.concatenate([total[:rows, 2 * rows :], rest], axis=1)


def call(kernel, name, grant, outs, inputs, scratch=()):
    return pl.pallas_call(
        kernel,
        out_shape=[jax.ShapeDtypeStruct(shape, dtype) for shape, dtype in outs],
        in_specs=[VMEM] * len(inputs),
        out_specs=[VMEM] * len(outs),
        scratch_shapes=scratch,
        compiler_params=pltpu.CompilerParams(vmem_limit_bytes=grant * 2**20),
        name=name,
    )(*inputs)


def on_device(vectors, coeffs):
    core = lax.axis_index("core")
    count, rows, nao = vectors.shape
    wide = coeffs.shape[2]
    half = wide // 2
    tall = 2 * rows + 8
    deep = 4 * rows + 16

    other_vectors = lax.ppermute(vectors, "core", SWAP)
    own = lax.dynamic_index_in_dim(coeffs, core, 0, keepdims=False)
    full = lax.all_to_all(jnp.broadcast_to(own[None], (32, rows, wide)), FAR, 0, 0, tiled=True).reshape(nao, wide)

    shape = (8, 2, 2, tall, half)
    (pieces,) = call(
        transform_kernel,
        "half_transform",
        16,
        [(shape, bf16)],
        (full, vectors, other_vectors, own),
    )
    got = lax.all_to_all(pieces.reshape(32, tall, half), FAR, 0, 0, tiled=True)
    got_other = lax.ppermute(got, "core", SWAP)

    scratch = [pltpu.VMEM((32 * rows, 2 * wide), bf16), pltpu.VMEM((16 * rows, 2 * wide), bf16)]
    (parts,) = call(
        exchange_kernel,
        "exchange_quarter",
        24,
        [((8, deep, 16 * rows), bf16)],
        (got.reshape(shape), got_other.reshape(shape), vectors, other_vectors),
        scratch,
    )
    parts = lax.all_to_all(parts, NEAR, 0, 0, tiled=True)
    packed, coulomb = call(
        near_sum_kernel, "near_sum", 12, [((16, rows + rows // 2, 128), bf16), ((rows, 2 * rows), f32)], (parts,)
    )
    packed = lax.all_to_all(packed, SUMS, 0, 0, tiled=True)
    (exchange,) = call(far_sum_kernel, "far_sum", 4, [((2, rows, 2 * rows), f32)], (packed,))
    return exchange, coulomb


def solution(mesh):
    fine = Mesh(mesh.devices.reshape(2, 4, 2, 8, 2, 2), ("zl", "x", "core", "y", "zb", "za"))
    chol = ("zl", "x", "core")
    return jax.shard_map(
        on_device,
        mesh=fine,
        in_specs=(P(chol, FAR, None), P(None, FAR, None)),
        out_specs=(P(None, FAR, chol), P(FAR, chol)),
        check_vma=False,
    )
```

```python
import jax
import jax.numpy as jnp
from jax import lax
from jax.experimental import pallas as pl
from jax.experimental.pallas import tpu as pltpu
from jax.sharding import Mesh
from jax.sharding import PartitionSpec as P

NEAR = ("zl", "x")
FAR = ("y", "zb", "za")
SUMS = ("y", "za")
SWAP = [(0, 1), (1, 0)]
f32, bf16 = jnp.float32, jnp.bfloat16
VMEM = pl.BlockSpec(memory_space=pltpu.VMEM)


def words(value):
    high = value.astype(bf16)
    return high, (value - high.astype(f32)).astype(bf16)


def vector_lanes(core, count, width):
    row = lax.broadcasted_iota(jnp.int32, (2 * count, width), 0)
    lane = lax.broadcasted_iota(jnp.int32, (2 * count, width), 1)
    return lane == jnp.where(core == 0, row, jnp.where(row < count, row + count, row - count))


def transform_kernel(full, mine, other, own, out):
    core = lax.axis_index("core")
    count, rows, nao = mine.shape
    wide = full.shape[1]
    half = wide // 2
    weight = own[...].astype(f32)
    terms = []
    for source, owner in ((mine, core), (other, 1 - core)):
        slab = jnp.dot(
            source[...].reshape(count * rows, nao), full[...], preferred_element_type=f32
        ).astype(bf16)
        for p in range(count):
            block = slab[p * rows : (p + 1) * rows]
            for zb in range(2):
                out[owner * (count // 2) + p // 2, zb, p % 2, 0:rows] = block[:, :half]
                out[owner * (count // 2) + p // 2, zb, p % 2, rows : 2 * rows] = block[:, half:]
            terms.append(jnp.sum(block.astype(f32) * weight, axis=0, keepdims=True))
    terms = jnp.sum(jnp.concatenate(terms), axis=1, keepdims=True)
    high, low = words(jnp.sum(jnp.where(vector_lanes(core, count, half), terms, 0.0), axis=0, keepdims=True))
    lines = lax.broadcasted_iota(jnp.int32, (8, half), 0)
    rider = jnp.where(lines == 0, high.astype(f32), jnp.where(lines == 1, low.astype(f32), 0.0))
    rider = rider.astype(bf16)
    for y in range(8):
        for zb in range(2):
            for za in range(2):
                out[y, zb, za, 2 * rows : 2 * rows + 8] = rider


def exchange_kernel(got, got_other, mine, other, out, column_side, row_side):
    core, zb = lax.axis_index("core"), lax.axis_index("zb")
    count, rows, nao = mine.shape
    half = got.shape[4]
    wide = 2 * half
    own_sign = jnp.where(core == 0, 1.0, -1.0).astype(bf16)
    other_sign = jnp.where(core == 0, -1.0, 1.0).astype(bf16)
    for y in range(8):
        for za in range(2):
            for h in range(2):
                own_at = slice(h * half, (h + 1) * half)
                other_at = slice(wide + h * half, wide + (h + 1) * half)
                part = slice(h * rows, (h + 1) * rows)
                at = pl.ds((2 * y + za) * rows, rows)
                row_side[at, own_at] = got[y, zb, za, part]
                row_side[at, other_at] = got_other[y, zb, za, part]
                own = got[y, core, za, part]
                other_part = got_other[y, core, za, part]
                at = pl.ds((4 * y + za) * rows, rows)
                column_side[at, own_at] = own
                column_side[at, other_at] = other_part
                at = pl.ds((4 * y + 2 + za) * rows, rows)
                column_side[at, own_at] = other_part * other_sign
                column_side[at, other_at] = own * own_sign

    riders = jnp.zeros((8, half), f32)
    for y in range(8):
        for b in range(2):
            for za in range(2):
                for source in (got, got_other):
                    riders += source[y, b, za, 2 * rows : 2 * rows + 8].astype(f32)
    weights = riders[0:1] + riders[1:2]
    weights = jnp.sum(jnp.where(vector_lanes(core, count, half), weights, 0.0), axis=1, keepdims=True)
    for part in range(3):
        at = pl.ds(part * 16, 16)
        total = jnp.zeros((16, nao), f32)
        for k, source in enumerate((mine, other)):
            for p in range(count):
                total += weights[k * count + p : k * count + p + 1] * source[p, at].astype(f32)
        for s in range(8):
            start = s * 4 * rows
            piece = jnp.where(
                core == 0, total[:, start : start + 2 * rows], total[:, start + 2 * rows : start + 4 * rows]
            )
            high, low = words(piece)
            gap = jnp.zeros((16, half - 2 * rows), bf16)
            out[s, 4 * rows : 4 * rows + 16, part * 256 : (part + 1) * 256] = jnp.concatenate(
                [high, gap, low, gap], axis=1
            )

    for n in range(3):
        block = lax.dot_general(
            column_side[...],
            row_side[n * 256 : (n + 1) * 256],
            (((1,), (1,)), ((), ())),
            preferred_element_type=f32,
        ).astype(bf16)
        for s in range(8):
            out[s, 0 : 4 * rows, n * 256 : (n + 1) * 256] = block[s * 4 * rows : (s + 1) * 4 * rows]


def near_sum_kernel(parts, out, tail):
    rows = parts.shape[2] // 16
    deep = 4 * rows
    tail[...] = jnp.sum(parts[:, deep : deep + 16].astype(f32), axis=0)
    for n in range(2):
        columns = slice(n * 8 * rows, (n + 1) * 8 * rows)
        turned = jnp.sum(parts[:, 0:deep, columns].astype(f32), axis=0).T
        for j in range(8):
            block = turned[j * rows : (j + 1) * rows]
            rest = jnp.concatenate([block[: rows // 2, 128:], block[rows // 2 :, 128:]], axis=1)
            out[n * 8 + j, 0:rows] = block[:, :128].astype(bf16)
            out[n * 8 + j, rows : rows + rows // 2] = rest.astype(bf16)


def far_sum_kernel(parts, tail, out, coulomb):
    rows = out.shape[1]
    for part in range(3):
        high = slice(part * 256, part * 256 + 2 * rows)
        low = slice(part * 256 + 128, part * 256 + 128 + 2 * rows)
        coulomb[part * 16 : (part + 1) * 16] = tail[:, high] + tail[:, low]
    total = jnp.sum(parts[...].astype(f32), axis=0)
    rest = jnp.concatenate([total[rows:, :64], total[rows:, 64:]], axis=0)
    out[0] = total[:rows, : 2 * rows]
    out[1] = jnp.concatenate([total[:rows, 2 * rows :], rest], axis=1)


def call(kernel, name, grant, outs, inputs, scratch=()):
    return pl.pallas_call(
        kernel,
        out_shape=[jax.ShapeDtypeStruct(shape, dtype) for shape, dtype in outs],
        in_specs=[VMEM] * len(inputs),
        out_specs=[VMEM] * len(outs),
        scratch_shapes=scratch,
        compiler_params=pltpu.CompilerParams(vmem_limit_bytes=grant * 2**20),
        name=name,
    )(*inputs)


def on_device(vectors, coeffs):
    core = lax.axis_index("core")
    count, rows, nao = vectors.shape
    wide = coeffs.shape[2]
    half = wide // 2
    tall = 2 * rows + 8
    deep = 4 * rows + 16

    other_vectors = lax.ppermute(vectors, "core", SWAP)
    own = lax.dynamic_index_in_dim(coeffs, core, 0, keepdims=False)
    full = lax.all_to_all(jnp.broadcast_to(own[None], (32, rows, wide)), FAR, 0, 0, tiled=True).reshape(nao, wide)

    shape = (8, 2, 2, tall, half)
    (pieces,) = call(
        transform_kernel,
        "half_transform",
        16,
        [(shape, bf16)],
        (full, vectors, other_vectors, own),
    )
    got = lax.all_to_all(pieces.reshape(32, tall, half), FAR, 0, 0, tiled=True)
    got_other = lax.ppermute(got, "core", SWAP)

    scratch = [pltpu.VMEM((32 * rows, 2 * wide), bf16), pltpu.VMEM((16 * rows, 2 * wide), bf16)]
    (parts,) = call(
        exchange_kernel,
        "exchange_quarter",
        24,
        [((8, deep, 16 * rows), bf16)],
        (got.reshape(shape), got_other.reshape(shape), vectors, other_vectors),
        scratch,
    )
    parts = lax.all_to_all(parts, NEAR, 0, 0, tiled=True)
    packed, tail = call(
        near_sum_kernel, "near_sum", 12, [((16, rows + rows // 2, 128), bf16), ((16, 16 * rows), f32)], (parts,)
    )
    packed = lax.all_to_all(packed, SUMS, 0, 0, tiled=True)
    return call(
        far_sum_kernel, "far_sum", 4, [((2, rows, 2 * rows), f32), ((rows, 2 * rows), f32)], (packed, tail)
    )


def solution(mesh):
    fine = Mesh(mesh.devices.reshape(2, 4, 2, 8, 2, 2), ("zl", "x", "core", "y", "zb", "za"))
    chol = ("zl", "x", "core")
    return jax.shard_map(
        on_device,
        mesh=fine,
        in_specs=(P(chol, FAR, None), P(None, FAR, None)),
        out_specs=(P(None, FAR, chol), P(FAR, chol)),
        check_vma=False,
    )
```

```python
import jax
import jax.numpy as jnp
from jax import lax
from jax.experimental import pallas as pl
from jax.experimental.pallas import tpu as pltpu
from jax.sharding import Mesh
from jax.sharding import PartitionSpec as P

NEAR = ("zl", "x")
FAR = ("y", "zb", "za")
SUMS = ("za", "y")
SWAP = [(0, 1), (1, 0)]
f32, bf16 = jnp.float32, jnp.bfloat16
VMEM = pl.BlockSpec(memory_space=pltpu.VMEM)


def words(value):
    high = value.astype(bf16)
    return high, (value - high.astype(f32)).astype(bf16)


def vector_lanes(core, count, width):
    row = lax.broadcasted_iota(jnp.int32, (2 * count, width), 0)
    lane = lax.broadcasted_iota(jnp.int32, (2 * count, width), 1)
    return lane == jnp.where(core == 0, row, jnp.where(row < count, row + count, row - count))


def transform_kernel(full, mine, other, own, out):
    core = lax.axis_index("core")
    count, rows, nao = mine.shape
    wide = full.shape[1]
    half = wide // 2
    weight = own[...].astype(f32)
    terms = []
    for source, owner in ((mine, core), (other, 1 - core)):
        slab = jnp.dot(
            source[...].reshape(count * rows, nao), full[...], preferred_element_type=f32
        ).astype(bf16)
        for p in range(count):
            block = slab[p * rows : (p + 1) * rows]
            for zb in range(2):
                out[owner * (count // 2) + p // 2, zb, p % 2, 0:rows] = block[:, :half]
                out[owner * (count // 2) + p // 2, zb, p % 2, rows : 2 * rows] = block[:, half:]
            terms.append(jnp.sum(block.astype(f32) * weight, axis=0, keepdims=True))
    terms = jnp.sum(jnp.concatenate(terms), axis=1, keepdims=True)
    high, low = words(jnp.sum(jnp.where(vector_lanes(core, count, half), terms, 0.0), axis=0, keepdims=True))
    lines = lax.broadcasted_iota(jnp.int32, (8, half), 0)
    rider = jnp.where(lines == 0, high.astype(f32), jnp.where(lines == 1, low.astype(f32), 0.0))
    rider = rider.astype(bf16)
    for y in range(8):
        for zb in range(2):
            for za in range(2):
                out[y, zb, za, 2 * rows : 2 * rows + 8] = rider


def exchange_kernel(got, got_other, mine, other, out, column_side, row_side):
    core, zb = lax.axis_index("core"), lax.axis_index("zb")
    count, rows, nao = mine.shape
    half = got.shape[4]
    wide = 2 * half
    own_sign = jnp.where(core == 0, 1.0, -1.0).astype(bf16)
    other_sign = jnp.where(core == 0, -1.0, 1.0).astype(bf16)
    for y in range(8):
        for za in range(2):
            for h in range(2):
                own_at = slice(h * half, (h + 1) * half)
                other_at = slice(wide + h * half, wide + (h + 1) * half)
                part = slice(h * rows, (h + 1) * rows)
                at = pl.ds((2 * y + za) * rows, rows)
                row_side[at, own_at] = got[y, zb, za, part]
                row_side[at, other_at] = got_other[y, zb, za, part]
                own = got[y, core, za, part]
                other_part = got_other[y, core, za, part]
                at = pl.ds((4 * y + za) * rows, rows)
                column_side[at, own_at] = own
                column_side[at, other_at] = other_part
                at = pl.ds((4 * y + 2 + za) * rows, rows)
                column_side[at, own_at] = other_part * other_sign
                column_side[at, other_at] = own * own_sign

    riders = jnp.zeros((8, half), f32)
    for y in range(8):
        for b in range(2):
            for za in range(2):
                for source in (got, got_other):
                    riders += source[y, b, za, 2 * rows : 2 * rows + 8].astype(f32)
    weights = riders[0:1] + riders[1:2]
    weights = jnp.sum(jnp.where(vector_lanes(core, count, half), weights, 0.0), axis=1, keepdims=True)
    for part in range(3):
        at = pl.ds(part * 16, 16)
        total = jnp.zeros((16, nao), f32)
        for k, source in enumerate((mine, other)):
            for p in range(count):
                total += weights[k * count + p : k * count + p + 1] * source[p, at].astype(f32)
        for s in range(8):
            start = s * 4 * rows
            piece = jnp.where(
                core == 0, total[:, start : start + 2 * rows], total[:, start + 2 * rows : start + 4 * rows]
            )
            high, low = words(piece)
            gap = jnp.zeros((16, half - 2 * rows), bf16)
            out[s, 4 * rows : 4 * rows + 16, part * 256 : (part + 1) * 256] = jnp.concatenate(
                [high, gap, low, gap], axis=1
            )

    for n in range(3):
        block = lax.dot_general(
            column_side[...],
            row_side[n * 256 : (n + 1) * 256],
            (((1,), (1,)), ((), ())),
            preferred_element_type=f32,
        ).astype(bf16)
        for s in range(8):
            out[s, 0 : 4 * rows, n * 256 : (n + 1) * 256] = block[s * 4 * rows : (s + 1) * 4 * rows]


def near_sum_kernel(parts, out, tail):
    rows = parts.shape[2] // 16
    deep = 4 * rows
    tail[...] = jnp.sum(parts[:, deep : deep + 16].astype(f32), axis=0)
    for n in range(2):
        columns = slice(n * 8 * rows, (n + 1) * 8 * rows)
        turned = jnp.sum(parts[:, 0:deep, columns].astype(f32), axis=0).T
        for j in range(8):
            block = turned[j * rows : (j + 1) * rows]
            rest = jnp.concatenate([block[: rows // 2, 128:], block[rows // 2 :, 128:]], axis=1)
            at = j % 2 * 8 + n * 4 + j // 2
            out[at, 0:rows] = block[:, :128].astype(bf16)
            out[at, rows : rows + rows // 2] = rest.astype(bf16)


def far_sum_kernel(parts, tail, out, coulomb):
    rows = out.shape[1]
    for part in range(3):
        high = slice(part * 256, part * 256 + 2 * rows)
        low = slice(part * 256 + 128, part * 256 + 128 + 2 * rows)
        coulomb[part * 16 : (part + 1) * 16] = tail[:, high] + tail[:, low]
    total = jnp.sum(parts[...].astype(f32), axis=0)
    rest = jnp.concatenate([total[rows:, :64], total[rows:, 64:]], axis=0)
    out[0] = total[:rows, : 2 * rows]
    out[1] = jnp.concatenate([total[:rows, 2 * rows :], rest], axis=1)


def call(kernel, name, grant, outs, inputs, scratch=()):
    return pl.pallas_call(
        kernel,
        out_shape=[jax.ShapeDtypeStruct(shape, dtype) for shape, dtype in outs],
        in_specs=[VMEM] * len(inputs),
        out_specs=[VMEM] * len(outs),
        scratch_shapes=scratch,
        compiler_params=pltpu.CompilerParams(vmem_limit_bytes=grant * 2**20),
        name=name,
    )(*inputs)


def on_device(vectors, coeffs):
    core = lax.axis_index("core")
    count, rows, nao = vectors.shape
    wide = coeffs.shape[2]
    half = wide // 2
    tall = 2 * rows + 8
    deep = 4 * rows + 16

    other_vectors = lax.ppermute(vectors, "core", SWAP)
    own = lax.dynamic_index_in_dim(coeffs, core, 0, keepdims=False)
    full = lax.all_to_all(jnp.broadcast_to(own[None], (32, rows, wide)), FAR, 0, 0, tiled=True).reshape(nao, wide)

    shape = (8, 2, 2, tall, half)
    (pieces,) = call(
        transform_kernel,
        "half_transform",
        16,
        [(shape, bf16)],
        (full, vectors, other_vectors, own),
    )
    got = lax.all_to_all(pieces.reshape(32, tall, half), FAR, 0, 0, tiled=True)
    got_other = lax.ppermute(got, "core", SWAP)

    scratch = [pltpu.VMEM((32 * rows, 2 * wide), bf16), pltpu.VMEM((16 * rows, 2 * wide), bf16)]
    (parts,) = call(
        exchange_kernel,
        "exchange_quarter",
        24,
        [((8, deep, 16 * rows), bf16)],
        (got.reshape(shape), got_other.reshape(shape), vectors, other_vectors),
        scratch,
    )
    parts = lax.all_to_all(parts, NEAR, 0, 0, tiled=True)
    packed, tail = call(
        near_sum_kernel, "near_sum", 12, [((16, rows + rows // 2, 128), bf16), ((16, 16 * rows), f32)], (parts,)
    )
    packed = lax.all_to_all(packed, SUMS, 0, 0, tiled=True)
    return call(
        far_sum_kernel, "far_sum", 4, [((2, rows, 2 * rows), f32), ((rows, 2 * rows), f32)], (packed, tail)
    )


def solution(mesh):
    fine = Mesh(mesh.devices.reshape(2, 4, 2, 8, 2, 2), ("zl", "x", "core", "y", "zb", "za"))
    chol = ("zl", "x", "core")
    return jax.shard_map(
        on_device,
        mesh=fine,
        in_specs=(P(chol, FAR, None), P(None, FAR, None)),
        out_specs=(P(None, FAR, chol), P(FAR, chol)),
        check_vma=False,
    )
```

```python
import jax
import jax.numpy as jnp
from jax import lax
from jax.experimental import pallas as pl
from jax.experimental.pallas import tpu as pltpu
from jax.sharding import Mesh
from jax.sharding import PartitionSpec as P

NEAR = ("zl", "x")
FAR = ("y", "zb", "za")
SUMS = ("za", "y")
SWAP = [(0, 1), (1, 0)]
f32, bf16 = jnp.float32, jnp.bfloat16
VMEM = pl.BlockSpec(memory_space=pltpu.VMEM)


def words(value):
    high = value.astype(bf16)
    return high, (value - high.astype(f32)).astype(bf16)


def packed_words(block):
    high = block.astype(bf16).astype(f32)
    both = jnp.concatenate([high, block - high])
    rest = jnp.concatenate([both[72:, 32 * k : 32 * (k + 1)] for k in range(3)])
    return jnp.concatenate([both[:72], rest], axis=1).astype(bf16)


def unpacked_words(block):
    rest = jnp.concatenate([block[24 * k : 24 * (k + 1), 96:] for k in range(3)], axis=1)
    both = jnp.concatenate([block[:, :96], rest])
    return both[:48] + both[48:]


def vector_lanes(core, count, width):
    row = lax.broadcasted_iota(jnp.int32, (2 * count, width), 0)
    lane = lax.broadcasted_iota(jnp.int32, (2 * count, width), 1)
    return lane == jnp.where(core == 0, row, jnp.where(row < count, row + count, row - count))


def transform_kernel(full, mine, other, own, out):
    core = lax.axis_index("core")
    count, rows, nao = mine.shape
    wide = full.shape[1]
    half = wide // 2
    weight = own[...].astype(f32)
    terms = []
    for source, owner in ((mine, core), (other, 1 - core)):
        slab = jnp.dot(
            source[...].reshape(count * rows, nao), full[...], preferred_element_type=f32
        ).astype(bf16)
        for p in range(count):
            block = slab[p * rows : (p + 1) * rows]
            for zb in range(2):
                out[owner * (count // 2) + p // 2, zb, p % 2, 0:rows] = block[:, :half]
                out[owner * (count // 2) + p // 2, zb, p % 2, rows : 2 * rows] = block[:, half:]
            terms.append(jnp.sum(block.astype(f32) * weight, axis=0, keepdims=True))
    terms = jnp.sum(jnp.concatenate(terms), axis=1, keepdims=True)
    high, low = words(jnp.sum(jnp.where(vector_lanes(core, count, half), terms, 0.0), axis=0, keepdims=True))
    lines = lax.broadcasted_iota(jnp.int32, (8, half), 0)
    rider = jnp.where(lines == 0, high.astype(f32), jnp.where(lines == 1, low.astype(f32), 0.0))
    rider = rider.astype(bf16)
    for y in range(8):
        for zb in range(2):
            for za in range(2):
                out[y, zb, za, 2 * rows : 2 * rows + 8] = rider


def exchange_kernel(got, got_other, mine, other, out, column_side, row_side):
    core, zb = lax.axis_index("core"), lax.axis_index("zb")
    count, rows, nao = mine.shape
    half = got.shape[4]
    wide = 2 * half
    own_sign = jnp.where(core == 0, 1.0, -1.0).astype(bf16)
    other_sign = jnp.where(core == 0, -1.0, 1.0).astype(bf16)
    for y in range(8):
        for za in range(2):
            for h in range(2):
                own_at = slice(h * half, (h + 1) * half)
                other_at = slice(wide + h * half, wide + (h + 1) * half)
                part = slice(h * rows, (h + 1) * rows)
                at = pl.ds((2 * y + za) * rows, rows)
                row_side[at, own_at] = got[y, zb, za, part]
                row_side[at, other_at] = got_other[y, zb, za, part]
                own = got[y, core, za, part]
                other_part = got_other[y, core, za, part]
                at = pl.ds((4 * y + za) * rows, rows)
                column_side[at, own_at] = own
                column_side[at, other_at] = other_part
                at = pl.ds((4 * y + 2 + za) * rows, rows)
                column_side[at, own_at] = other_part * other_sign
                column_side[at, other_at] = own * own_sign

    riders = jnp.zeros((8, half), f32)
    for y in range(8):
        for b in range(2):
            for za in range(2):
                for source in (got, got_other):
                    riders += source[y, b, za, 2 * rows : 2 * rows + 8].astype(f32)
    weights = riders[0:1] + riders[1:2]
    weights = jnp.sum(jnp.where(vector_lanes(core, count, half), weights, 0.0), axis=1, keepdims=True)
    shares = [[] for _ in range(8)]
    for part in range(3):
        at = pl.ds(part * 16, 16)
        total = jnp.zeros((16, nao), f32)
        for k, source in enumerate((mine, other)):
            for p in range(count):
                total += weights[k * count + p : k * count + p + 1] * source[p, at].astype(f32)
        for s in range(8):
            start = s * 4 * rows
            piece = jnp.where(
                core == 0, total[:, start : start + 2 * rows], total[:, start + 2 * rows : start + 4 * rows]
            )
            shares[s].append(piece)
    for s in range(8):
        out[s, 24 * rows :] = packed_words(jnp.concatenate(shares[s]))

    for n in range(3):
        block = lax.dot_general(
            column_side[...],
            row_side[n * 256 : (n + 1) * 256],
            (((1,), (1,)), ((), ())),
            preferred_element_type=f32,
        ).astype(bf16)
        for s in range(8):
            for g in range(2):
                at = pl.ds((2 * n + g) * 4 * rows, 4 * rows)
                out[s, at] = block[s * 4 * rows : (s + 1) * 4 * rows, g * 128 : (g + 1) * 128]


def near_sum_kernel(parts, out, tail):
    rows = out.shape[1] // 3 * 2
    deep = 4 * rows
    tail[...] = jnp.sum(parts[:, 6 * deep :].astype(f32), axis=0)
    for n in range(2):
        groups = range(3 * n, 3 * n + 3)
        turned = jnp.concatenate(
            [jnp.sum(parts[:, g * deep : (g + 1) * deep].astype(f32), axis=0).T for g in groups]
        )
        for j in range(8):
            block = turned[j * rows : (j + 1) * rows]
            rest = jnp.concatenate([block[: rows // 2, 128:], block[rows // 2 :, 128:]], axis=1)
            at = j % 2 * 8 + n * 4 + j // 2
            out[at, 0:rows] = block[:, :128].astype(bf16)
            out[at, rows : rows + rows // 2] = rest.astype(bf16)


def far_sum_kernel(parts, tail, out, coulomb):
    rows = out.shape[1]
    coulomb[...] = unpacked_words(tail[...])
    total = jnp.sum(parts[...].astype(f32), axis=0)
    rest = jnp.concatenate([total[rows:, :64], total[rows:, 64:]], axis=0)
    out[0] = total[:rows, : 2 * rows]
    out[1] = jnp.concatenate([total[:rows, 2 * rows :], rest], axis=1)


def call(kernel, name, grant, outs, inputs, scratch=()):
    return pl.pallas_call(
        kernel,
        out_shape=[jax.ShapeDtypeStruct(shape, dtype) for shape, dtype in outs],
        in_specs=[VMEM] * len(inputs),
        out_specs=[VMEM] * len(outs),
        scratch_shapes=scratch,
        compiler_params=pltpu.CompilerParams(vmem_limit_bytes=grant * 2**20),
        name=name,
    )(*inputs)


def on_device(vectors, coeffs):
    core = lax.axis_index("core")
    count, rows, nao = vectors.shape
    wide = coeffs.shape[2]
    half = wide // 2
    tall = 2 * rows + 8
    deep = 24 * rows + 72

    other_vectors = lax.ppermute(vectors, "core", SWAP)
    own = lax.dynamic_index_in_dim(coeffs, core, 0, keepdims=False)
    full = lax.all_to_all(jnp.broadcast_to(own[None], (32, rows, wide)), FAR, 0, 0, tiled=True).reshape(nao, wide)

    shape = (8, 2, 2, tall, half)
    (pieces,) = call(
        transform_kernel,
        "half_transform",
        16,
        [(shape, bf16)],
        (full, vectors, other_vectors, own),
    )
    got = lax.all_to_all(pieces.reshape(32, tall, half), FAR, 0, 0, tiled=True)
    got_other = lax.ppermute(got, "core", SWAP)

    scratch = [pltpu.VMEM((32 * rows, 2 * wide), bf16), pltpu.VMEM((16 * rows, 2 * wide), bf16)]
    (parts,) = call(
        exchange_kernel,
        "exchange_quarter",
        24,
        [((8, deep, 128), bf16)],
        (got.reshape(shape), got_other.reshape(shape), vectors, other_vectors),
        scratch,
    )
    parts = lax.all_to_all(parts, NEAR, 0, 0, tiled=True)
    packed, tail = call(
        near_sum_kernel, "near_sum", 12, [((16, rows + rows // 2, 128), bf16), ((72, 128), f32)], (parts,)
    )
    packed = lax.all_to_all(packed, SUMS, 0, 0, tiled=True)
    return call(
        far_sum_kernel, "far_sum", 4, [((2, rows, 2 * rows), f32), ((rows, 2 * rows), f32)], (packed, tail)
    )


def solution(mesh):
    fine = Mesh(mesh.devices.reshape(2, 4, 2, 8, 2, 2), ("zl", "x", "core", "y", "zb", "za"))
    chol = ("zl", "x", "core")
    return jax.shard_map(
        on_device,
        mesh=fine,
        in_specs=(P(chol, FAR, None), P(None, FAR, None)),
        out_specs=(P(None, FAR, chol), P(FAR, chol)),
        check_vma=False,
    )
```

```python
import jax
import jax.numpy as jnp
from jax import lax
from jax.experimental import pallas as pl
from jax.experimental.pallas import tpu as pltpu
from jax.sharding import Mesh
from jax.sharding import PartitionSpec as P

NEAR = ("zl", "x")
FAR = ("y", "zb", "za")
SUMS = ("za", "y")
SWAP = [(0, 1), (1, 0)]
f32, bf16 = jnp.float32, jnp.bfloat16
VMEM = pl.BlockSpec(memory_space=pltpu.VMEM)


def words(value):
    high = value.astype(bf16)
    return high, (value - high.astype(f32)).astype(bf16)


def packed_words(block):
    high = block.astype(bf16).astype(f32)
    low = block - high
    rest = jnp.concatenate([low[:24, 32:], low[24:, 32:]], axis=1)
    return jnp.concatenate([jnp.concatenate([high, low[:, :32]], axis=1), rest]).astype(bf16)


def unpacked_words(block):
    rest = jnp.concatenate([block[48:, :64], block[48:, 64:]])
    return block[:48, :96] + jnp.concatenate([block[:48, 96:], rest], axis=1)


def vector_lanes(core, count, width):
    row = lax.broadcasted_iota(jnp.int32, (2 * count, width), 0)
    lane = lax.broadcasted_iota(jnp.int32, (2 * count, width), 1)
    return lane == jnp.where(core == 0, row, jnp.where(row < count, row + count, row - count))


def transform_kernel(full, mine, other, own, out):
    core = lax.axis_index("core")
    count, rows, nao = mine.shape
    wide = full.shape[1]
    half = wide // 2
    weight = own[...].astype(f32)
    terms = []
    for source, owner in ((mine, core), (other, 1 - core)):
        slab = jnp.dot(
            source[...].reshape(count * rows, nao), full[...], preferred_element_type=f32
        ).astype(bf16)
        for p in range(count):
            block = slab[p * rows : (p + 1) * rows]
            for zb in range(2):
                out[owner * (count // 2) + p // 2, zb, p % 2, 0:rows] = block[:, :half]
                out[owner * (count // 2) + p // 2, zb, p % 2, rows : 2 * rows] = block[:, half:]
            terms.append(jnp.sum(block.astype(f32) * weight, axis=0, keepdims=True))
    terms = jnp.sum(jnp.concatenate(terms), axis=1, keepdims=True)
    high, low = words(jnp.sum(jnp.where(vector_lanes(core, count, half), terms, 0.0), axis=0, keepdims=True))
    lines = lax.broadcasted_iota(jnp.int32, (8, half), 0)
    rider = jnp.where(lines == 0, high.astype(f32), jnp.where(lines == 1, low.astype(f32), 0.0))
    rider = rider.astype(bf16)
    for y in range(8):
        for zb in range(2):
            for za in range(2):
                out[y, zb, za, 2 * rows : 2 * rows + 8] = rider


def exchange_kernel(got, got_other, mine, other, out, column_side, row_side):
    core, zb = lax.axis_index("core"), lax.axis_index("zb")
    count, rows, nao = mine.shape
    half = got.shape[4]
    wide = 2 * half
    own_sign = jnp.where(core == 0, 1.0, -1.0).astype(bf16)
    other_sign = jnp.where(core == 0, -1.0, 1.0).astype(bf16)
    for y in range(8):
        for za in range(2):
            for h in range(2):
                own_at = slice(h * half, (h + 1) * half)
                other_at = slice(wide + h * half, wide + (h + 1) * half)
                part = slice(h * rows, (h + 1) * rows)
                at = pl.ds((2 * y + za) * rows, rows)
                row_side[at, own_at] = got[y, zb, za, part]
                row_side[at, other_at] = got_other[y, zb, za, part]
                own = got[y, core, za, part]
                other_part = got_other[y, core, za, part]
                at = pl.ds((4 * y + za) * rows, rows)
                column_side[at, own_at] = own
                column_side[at, other_at] = other_part
                at = pl.ds((4 * y + 2 + za) * rows, rows)
                column_side[at, own_at] = other_part * other_sign
                column_side[at, other_at] = own * own_sign

    riders = jnp.zeros((8, half), f32)
    for y in range(8):
        for b in range(2):
            for za in range(2):
                for source in (got, got_other):
                    riders += source[y, b, za, 2 * rows : 2 * rows + 8].astype(f32)
    weights = riders[0:1] + riders[1:2]
    weights = jnp.sum(jnp.where(vector_lanes(core, count, half), weights, 0.0), axis=1, keepdims=True)
    shares = [[] for _ in range(8)]
    for part in range(3):
        at = pl.ds(part * 16, 16)
        total = jnp.zeros((16, nao), f32)
        for k, source in enumerate((mine, other)):
            for p in range(count):
                total += weights[k * count + p : k * count + p + 1] * source[p, at].astype(f32)
        total = jnp.where(core == 0, total, pltpu.roll(total, nao - 2 * rows, 1))
        for s in range(8):
            shares[s].append(total[:, s * 4 * rows : s * 4 * rows + 2 * rows])
    for s in range(8):
        out[s, 24 * rows :] = packed_words(jnp.concatenate(shares[s]))

    for n in range(3):
        block = lax.dot_general(
            column_side[...],
            row_side[n * 256 : (n + 1) * 256],
            (((1,), (1,)), ((), ())),
            preferred_element_type=f32,
        ).astype(bf16)
        for s in range(8):
            for g in range(2):
                at = pl.ds((2 * n + g) * 4 * rows, 4 * rows)
                out[s, at] = block[s * 4 * rows : (s + 1) * 4 * rows, g * 128 : (g + 1) * 128]


def near_sum_kernel(parts, out, tail):
    rows = out.shape[1] // 3 * 2
    deep = 4 * rows
    tail[...] = jnp.sum(parts[:, 6 * deep :].astype(f32), axis=0)
    for n in range(2):
        groups = range(3 * n, 3 * n + 3)
        turned = jnp.concatenate(
            [jnp.sum(parts[:, g * deep : (g + 1) * deep].astype(f32), axis=0).T for g in groups]
        )
        for j in range(8):
            block = turned[j * rows : (j + 1) * rows]
            rest = jnp.concatenate([block[: rows // 2, 128:], block[rows // 2 :, 128:]], axis=1)
            at = j % 2 * 8 + n * 4 + j // 2
            out[at, 0:rows] = block[:, :128].astype(bf16)
            out[at, rows : rows + rows // 2] = rest.astype(bf16)


def far_sum_kernel(parts, tail, out, coulomb):
    rows = out.shape[1]
    coulomb[...] = unpacked_words(tail[...])
    total = jnp.sum(parts[...].astype(f32), axis=0)
    rest = jnp.concatenate([total[rows:, :64], total[rows:, 64:]], axis=0)
    out[0] = total[:rows, : 2 * rows]
    out[1] = jnp.concatenate([total[:rows, 2 * rows :], rest], axis=1)


def call(kernel, name, grant, outs, inputs, scratch=()):
    return pl.pallas_call(
        kernel,
        out_shape=[jax.ShapeDtypeStruct(shape, dtype) for shape, dtype in outs],
        in_specs=[VMEM] * len(inputs),
        out_specs=[VMEM] * len(outs),
        scratch_shapes=scratch,
        compiler_params=pltpu.CompilerParams(vmem_limit_bytes=grant * 2**20),
        name=name,
    )(*inputs)


def on_device(vectors, coeffs):
    core = lax.axis_index("core")
    count, rows, nao = vectors.shape
    wide = coeffs.shape[2]
    half = wide // 2
    tall = 2 * rows + 8
    deep = 24 * rows + 72

    other_vectors = lax.ppermute(vectors, "core", SWAP)
    own = lax.dynamic_index_in_dim(coeffs, core, 0, keepdims=False)
    full = lax.all_to_all(jnp.broadcast_to(own[None], (32, rows, wide)), FAR, 0, 0, tiled=True).reshape(nao, wide)

    shape = (8, 2, 2, tall, half)
    (pieces,) = call(
        transform_kernel,
        "half_transform",
        16,
        [(shape, bf16)],
        (full, vectors, other_vectors, own),
    )
    got = lax.all_to_all(pieces.reshape(32, tall, half), FAR, 0, 0, tiled=True)
    got_other = lax.ppermute(got, "core", SWAP)

    scratch = [pltpu.VMEM((32 * rows, 2 * wide), bf16), pltpu.VMEM((16 * rows, 2 * wide), bf16)]
    (parts,) = call(
        exchange_kernel,
        "exchange_quarter",
        24,
        [((8, deep, 128), bf16)],
        (got.reshape(shape), got_other.reshape(shape), vectors, other_vectors),
        scratch,
    )
    parts = lax.all_to_all(parts, NEAR, 0, 0, tiled=True)
    packed, tail = call(
        near_sum_kernel, "near_sum", 12, [((16, rows + rows // 2, 128), bf16), ((72, 128), f32)], (parts,)
    )
    packed = lax.all_to_all(packed, SUMS, 0, 0, tiled=True)
    return call(
        far_sum_kernel, "far_sum", 4, [((2, rows, 2 * rows), f32), ((rows, 2 * rows), f32)], (packed, tail)
    )


def solution(mesh):
    fine = Mesh(mesh.devices.reshape(2, 4, 2, 8, 2, 2), ("zl", "x", "core", "y", "zb", "za"))
    chol = ("zl", "x", "core")
    return jax.shard_map(
        on_device,
        mesh=fine,
        in_specs=(P(chol, FAR, None), P(None, FAR, None)),
        out_specs=(P(None, FAR, chol), P(FAR, chol)),
        check_vma=False,
    )
```

```python
import jax
import jax.numpy as jnp
from jax import lax
from jax.experimental import pallas as pl
from jax.experimental.pallas import tpu as pltpu
from jax.sharding import Mesh
from jax.sharding import PartitionSpec as P

NEAR = ("zl", "x")
FAR = ("y", "zb", "za")
SUMS = ("za", "y")
SWAP = [(0, 1), (1, 0)]
f32, bf16 = jnp.float32, jnp.bfloat16
VMEM = pl.BlockSpec(memory_space=pltpu.VMEM)


def words(value):
    high = value.astype(bf16)
    return high, (value - high.astype(f32)).astype(bf16)


def packed_words(block):
    high = block.astype(bf16).astype(f32)
    low = block - high
    rest = jnp.concatenate([low[:24, 32:], low[24:, 32:]], axis=1)
    return jnp.concatenate([jnp.concatenate([high, low[:, :32]], axis=1), rest]).astype(bf16)


def unpacked_words(block):
    rest = jnp.concatenate([block[48:, :64], block[48:, 64:]])
    return block[:48, :96] + jnp.concatenate([block[:48, 96:], rest], axis=1)


def vector_lanes(core, count, width):
    row = lax.broadcasted_iota(jnp.int32, (2 * count, width), 0)
    lane = lax.broadcasted_iota(jnp.int32, (2 * count, width), 1)
    return lane == jnp.where(core == 0, row, jnp.where(row < count, row + count, row - count))


def transform_kernel(full, mine, other, own, out):
    core = lax.axis_index("core")
    count, rows, nao = mine.shape
    wide = full.shape[1]
    half = wide // 2
    weight = own[...].astype(f32)
    terms = []
    both = jnp.concatenate([source[...].reshape(count * rows, nao) for source in (mine, other)])
    slab = jnp.dot(both, full[...], preferred_element_type=f32).astype(bf16)
    for k, owner in enumerate((core, 1 - core)):
        for p in range(count):
            block = slab[(k * count + p) * rows : (k * count + p + 1) * rows]
            for zb in range(2):
                out[owner * (count // 2) + p // 2, zb, p % 2, 0:rows] = block[:, :half]
                out[owner * (count // 2) + p // 2, zb, p % 2, rows : 2 * rows] = block[:, half:]
            terms.append(jnp.sum(block.astype(f32) * weight, axis=0, keepdims=True))
    terms = jnp.sum(jnp.concatenate(terms), axis=1, keepdims=True)
    high, low = words(jnp.sum(jnp.where(vector_lanes(core, count, half), terms, 0.0), axis=0, keepdims=True))
    lines = lax.broadcasted_iota(jnp.int32, (8, half), 0)
    rider = jnp.where(lines == 0, high.astype(f32), jnp.where(lines == 1, low.astype(f32), 0.0))
    rider = rider.astype(bf16)
    for y in range(8):
        for zb in range(2):
            for za in range(2):
                out[y, zb, za, 2 * rows : 2 * rows + 8] = rider


def exchange_kernel(got, got_other, mine, other, out, column_side, row_side):
    core, zb = lax.axis_index("core"), lax.axis_index("zb")
    count, rows, nao = mine.shape
    half = got.shape[4]
    wide = 2 * half
    own_sign = jnp.where(core == 0, 1.0, -1.0).astype(bf16)
    other_sign = jnp.where(core == 0, -1.0, 1.0).astype(bf16)
    for y in range(8):
        for za in range(2):
            for h in range(2):
                own_at = slice(h * half, (h + 1) * half)
                other_at = slice(wide + h * half, wide + (h + 1) * half)
                part = slice(h * rows, (h + 1) * rows)
                at = pl.ds((2 * y + za) * rows, rows)
                row_side[at, own_at] = got[y, zb, za, part]
                row_side[at, other_at] = got_other[y, zb, za, part]
                own = got[y, core, za, part]
                other_part = got_other[y, core, za, part]
                at = pl.ds((4 * y + za) * rows, rows)
                column_side[at, own_at] = own
                column_side[at, other_at] = other_part
                at = pl.ds((4 * y + 2 + za) * rows, rows)
                column_side[at, own_at] = other_part * other_sign
                column_side[at, other_at] = own * own_sign

    riders = jnp.zeros((8, half), f32)
    for y in range(8):
        for b in range(2):
            for za in range(2):
                for source in (got, got_other):
                    riders += source[y, b, za, 2 * rows : 2 * rows + 8].astype(f32)
    weights = riders[0:1] + riders[1:2]
    weights = jnp.sum(jnp.where(vector_lanes(core, count, half), weights, 0.0), axis=1, keepdims=True)
    shares = [[] for _ in range(8)]
    for part in range(3):
        at = pl.ds(part * 16, 16)
        total = jnp.zeros((16, nao), f32)
        for k, source in enumerate((mine, other)):
            for p in range(count):
                total += weights[k * count + p : k * count + p + 1] * source[p, at].astype(f32)
        total = jnp.where(core == 0, total, pltpu.roll(total, nao - 2 * rows, 1))
        for s in range(8):
            shares[s].append(total[:, s * 4 * rows : s * 4 * rows + 2 * rows])
    for s in range(8):
        out[s, 24 * rows :] = packed_words(jnp.concatenate(shares[s]))

    for n in range(3):
        block = lax.dot_general(
            column_side[...],
            row_side[n * 256 : (n + 1) * 256],
            (((1,), (1,)), ((), ())),
            preferred_element_type=f32,
        ).astype(bf16)
        for s in range(8):
            for g in range(2):
                at = pl.ds((2 * n + g) * 4 * rows, 4 * rows)
                out[s, at] = block[s * 4 * rows : (s + 1) * 4 * rows, g * 128 : (g + 1) * 128]


def near_sum_kernel(parts, out, tail):
    rows = out.shape[1] // 3 * 2
    deep = 4 * rows
    tail[...] = jnp.sum(parts[:, 6 * deep :].astype(f32), axis=0)
    for n in range(2):
        groups = range(3 * n, 3 * n + 3)
        turned = jnp.concatenate(
            [jnp.sum(parts[:, g * deep : (g + 1) * deep].astype(f32), axis=0).T for g in groups]
        )
        for j in range(8):
            block = turned[j * rows : (j + 1) * rows]
            rest = jnp.concatenate([block[: rows // 2, 128:], block[rows // 2 :, 128:]], axis=1)
            at = j % 2 * 8 + n * 4 + j // 2
            out[at, 0:rows] = block[:, :128].astype(bf16)
            out[at, rows : rows + rows // 2] = rest.astype(bf16)


def far_sum_kernel(parts, tail, out, coulomb):
    rows = out.shape[1]
    coulomb[...] = unpacked_words(tail[...])
    total = jnp.sum(parts[...].astype(f32), axis=0)
    rest = jnp.concatenate([total[rows:, :64], total[rows:, 64:]], axis=0)
    out[0] = total[:rows, : 2 * rows]
    out[1] = jnp.concatenate([total[:rows, 2 * rows :], rest], axis=1)


def call(kernel, name, grant, outs, inputs, scratch=()):
    return pl.pallas_call(
        kernel,
        out_shape=[jax.ShapeDtypeStruct(shape, dtype) for shape, dtype in outs],
        in_specs=[VMEM] * len(inputs),
        out_specs=[VMEM] * len(outs),
        scratch_shapes=scratch,
        compiler_params=pltpu.CompilerParams(vmem_limit_bytes=grant * 2**20),
        name=name,
    )(*inputs)


def on_device(vectors, coeffs):
    core = lax.axis_index("core")
    count, rows, nao = vectors.shape
    wide = coeffs.shape[2]
    half = wide // 2
    tall = 2 * rows + 8
    deep = 24 * rows + 72

    other_vectors = lax.ppermute(vectors, "core", SWAP)
    own = lax.dynamic_index_in_dim(coeffs, core, 0, keepdims=False)
    full = lax.all_to_all(jnp.broadcast_to(own[None], (32, rows, wide)), FAR, 0, 0, tiled=True).reshape(nao, wide)

    shape = (8, 2, 2, tall, half)
    (pieces,) = call(
        transform_kernel,
        "half_transform",
        16,
        [(shape, bf16)],
        (full, vectors, other_vectors, own),
    )
    got = lax.all_to_all(pieces.reshape(32, tall, half), FAR, 0, 0, tiled=True)
    got_other = lax.ppermute(got, "core", SWAP)

    scratch = [pltpu.VMEM((32 * rows, 2 * wide), bf16), pltpu.VMEM((16 * rows, 2 * wide), bf16)]
    (parts,) = call(
        exchange_kernel,
        "exchange_quarter",
        24,
        [((8, deep, 128), bf16)],
        (got.reshape(shape), got_other.reshape(shape), vectors, other_vectors),
        scratch,
    )
    parts = lax.all_to_all(parts, NEAR, 0, 0, tiled=True)
    packed, tail = call(
        near_sum_kernel, "near_sum", 12, [((16, rows + rows // 2, 128), bf16), ((72, 128), f32)], (parts,)
    )
    packed = lax.all_to_all(packed, SUMS, 0, 0, tiled=True)
    return call(
        far_sum_kernel, "far_sum", 4, [((2, rows, 2 * rows), f32), ((rows, 2 * rows), f32)], (packed, tail)
    )


def solution(mesh):
    fine = Mesh(mesh.devices.reshape(2, 4, 2, 8, 2, 2), ("zl", "x", "core", "y", "zb", "za"))
    chol = ("zl", "x", "core")
    return jax.shard_map(
        on_device,
        mesh=fine,
        in_specs=(P(chol, FAR, None), P(None, FAR, None)),
        out_specs=(P(None, FAR, chol), P(FAR, chol)),
        check_vma=False,
    )
```
